32 devices in a mesh: row: 8 (over z, x), feat: 4 (over y, core).
Axes of the slice: x: 2, y: 2, z: 4, core: 2. Of those that a mesh axis runs over, the one named last changes fastest.
Arguments:
- candidates: bfloat16 [512, 16384], P('row', 'feat'), may hold values from -48 to 48, as said below
- inv_factor: bfloat16 [16384, 16384], P('row', 'feat'), may hold values from -1.5 to 1.5, as said below
- weights: float32 [512], P('row'), may hold values from 0.01 to 0.1
- strata: int32 [512], P('row'), may hold values from 0 to 15, never falling along the last dimension, each value on 1 to 256 neighbouring positions
Outputs:
- new_weight: float32 [512], P('row')
- leverage: float32 [512], P('row')
- information: float32 [16384, 16384], P('row', 'feat')
The draws below stay inside these ranges and needn't reach their ends.
Inputs may be any that keep to these rules, and one draw needn't show every extreme that they name: `candidates`: row scales and column scales differ. `inv_factor`: zero above the diagonal, positive on the diagonal.
All inputs are finite; a program needn't handle non-finite values.
Results may differ from the reference program's by a relative error of at most 0.0029.
Values may be sent and summed in bfloat16 or wider, within the bound.
No kernel may reach another device: no remote copies, remote signals or barrier semaphores. Data moves between devices by JAX's collectives and lax.ppermute only.
A program may use at most 128 MiB of HBM per device.

```python
import math
import jax
import jax.numpy as jnp
import numpy as np
from jax import lax

FEATURES = 16384
ROWS = 512
STRATA = 16
MOST = 256


def draw_candidates(key, part):
    key_row, key_col, key_base = jax.random.split(key, 3)
    rising = jnp.exp(math.log(3.0) * jnp.arange(ROWS, dtype=jnp.float32) / ROWS)
    row_scale = rising * jnp.exp(jax.random.uniform(key_row, (ROWS,), jnp.float32, math.log(0.5), math.log(2.0)))
    col_scale = jnp.exp(jax.random.uniform(key_col, (FEATURES,), jnp.float32, math.log(0.5), math.log(2.0)))
    base_draw = jnp.clip(jax.random.normal(key_base, (ROWS, FEATURES), jnp.float32), -4.0, 4.0)
    return (row_scale[:, None] * col_scale[None, :] * base_draw).astype(jnp.bfloat16)


def draw_inv_factor(key, part):
    key_noise, key_diag = jax.random.split(key, 2)
    indices = jnp.arange(FEATURES, dtype=jnp.int32)
    spread = 0.8 / math.sqrt(FEATURES)
    noise_part = jnp.clip(jax.random.normal(key_noise, (FEATURES, FEATURES), jnp.float32), -4.0, 4.0) * spread
    diagonal = jnp.exp(jax.random.uniform(key_diag, (FEATURES,), jnp.float32, math.log(0.7), math.log(1.4)))
    below_diag = indices[:, None] > indices[None, :]
    on_diag = indices[:, None] == indices[None, :]
    filled = jnp.where(below_diag, noise_part, 0.0) + jnp.where(on_diag, diagonal[:, None], 0.0)
    return filled.astype(jnp.bfloat16)


def shard_levels(own_key, shape, cuts, least, top_value):
    factor_of, own = 1.0, jax.random.fold_in(own_key, 6)
    for position, shards_of in cuts:
        heights = jnp.exp(jax.random.uniform(jax.random.fold_in(own, position), (shards_of,), jnp.float32, least / len(cuts), top_value / len(cuts)))
        factor_of = factor_of * jnp.repeat(heights, shape[position] // shards_of).reshape([-1 if axis == position else 1 for axis in range(len(shape))])
    return factor_of


def split_up(number_of, total, limit, skew):
    portions = [(1 << 20) // math.isqrt(grade ** skew) + 1 for grade in range(2, number_of + 1)]
    rest, holding = total - limit - (number_of - 1), [1] * (number_of - 1)
    while rest > 0:
        movable = [i for i in range(number_of - 1) if holding[i] < limit]
        whole, remaining = sum([portions[i] for i in movable]), rest
        for i in movable:
            extra = min(limit - holding[i], max(1, remaining * portions[i] // whole), rest)
            holding[i] = holding[i] + extra
            rest = rest - extra
    return np.array([limit] + holding)


def uneven(key, number_of, total, bound, slope):
    if number_of == 2:
        one = jax.random.randint(key, (), max(1, total - bound), min(bound, total - 1) + 1)
        return jnp.stack([one, total - one])
    tallies = jnp.asarray(split_up(number_of, total, bound, slope), jnp.int32)
    twos = (number_of - 1) // 2
    source_of, sink = tallies[1:1 + 2 * twos:2], tallies[2:2 + 2 * twos:2]
    room = jnp.minimum(source_of - 1, bound - sink)
    moved = jax.random.randint(jax.random.fold_in(key, 1), (twos,), 0, 1 << 20) % (room + 1)
    tallies = tallies.at[1:1 + 2 * twos:2].set(source_of - moved).at[2:2 + 2 * twos:2].set(sink + moved)
    return tallies[jax.random.permutation(jax.random.fold_in(key, 2), number_of)]


def setup_inputs(seed: int = 0) -> dict:
    key_list = jax.random.split(jax.random.key(seed), 5)
    candidates = draw_candidates(jax.random.fold_in(key_list[4], 71), 0)
    inv_factor = draw_inv_factor(jax.random.fold_in(key_list[4], 71), 0)
    weights = jnp.clip(jnp.exp(math.log(0.1) - 2.3025851 * jax.random.uniform(key_list[2], (ROWS,), jnp.float32) ** shard_levels(key_list[2], (ROWS,), ((0, 8),), -0.2, 0.2)), 0.01, 0.1)
    strata = jnp.searchsorted(jnp.cumsum(uneven(key_list[3], STRATA, ROWS, MOST, 2)), jnp.arange(ROWS), side="right").astype(jnp.int32)
    return dict(candidates=candidates, inv_factor=inv_factor, weights=weights, strata=strata)


def reference(candidates, inv_factor, weights, strata):
    whitened = lax.dot_general(candidates, inv_factor, (((1,), (1,)), ((), ())), preferred_element_type=jnp.float32)
    raw_leverage = jnp.sum(whitened * whitened, axis=1)
    leverage = raw_leverage / FEATURES
    products = weights * raw_leverage
    stratum_product = jax.ops.segment_sum(products, strata, num_segments=STRATA)
    stratum_mass = jax.ops.segment_sum(weights, strata, num_segments=STRATA)
    stratum_ratio = stratum_mass / stratum_product
    new_weight = products * stratum_ratio[strata]
    weight_step = new_weight - weights
    scaled = (weight_step[:, None] * candidates.astype(jnp.float32)).astype(jnp.bfloat16)
    information = lax.dot_general(candidates, scaled, (((0,), (0,)), ((), ())), preferred_element_type=jnp.float32)
    return (new_weight, leverage, information)
```

```python
import jax
import jax.numpy as jnp
from jax import lax
from jax.sharding import PartitionSpec as P

BOTH = ("row", "feat")
HI = 4


def ring_order(count):
    return list(range(0, count, 2)) + list(range(1, count, 2))[::-1]


def ring_next(count):
    order = ring_order(count)
    return {order[i]: order[(i + 1) % count] for i in range(count)}


def tree_sum(values):
    values = list(values)
    while len(values) > 1:
        values = [values[i] + values[i + 1] for i in range(0, len(values), 2)]
    return values[0]


def make(mesh):
    rows_n, feats_n = mesh.shape["row"], mesh.shape["feat"]
    hi_n = HI
    lo_n = rows_n // hi_n
    pairs_row = [(r, f) for r in range(rows_n) for f in range(feats_n)]

    def perm(fn, keep=lambda r, f: True):
        out = []
        for r, f in pairs_row:
            if keep(r, f):
                r2, f2 = fn(r, f)
                out.append((r * feats_n + f, r2 * feats_n + f2))
        return out

    def send(x, pairs):
        return lax.ppermute(x, BOTH, pairs)

    hi_next, lo_next = ring_next(hi_n), ring_next(lo_n)
    hi_pairs = perm(lambda r, f: (hi_next[r // lo_n] * lo_n + r % lo_n, f))
    lo_pairs = perm(lambda r, f: (r // lo_n * lo_n + lo_next[r % lo_n], f))
    per_feat = rows_n // feats_n

    def root(r):
        return r // per_feat

    hi_order, lo_order = ring_order(hi_n), ring_order(lo_n)

    def source(r, k, s):
        h, l = r // lo_n, r % lo_n
        h2 = hi_order[(hi_order.index(h) - k) % hi_n]
        l2 = lo_order[(lo_order.index(l) - s) % lo_n]
        return h2 * lo_n + l2

    slots = [(k, s) for k in range(hi_n) for s in range(lo_n)]
    source_table = [[source(r, k, s) for k, s in slots] for r in range(rows_n)]

    def per_device(candidates, inv_factor, weights, strata):
        rows_dev, feat_block = candidates.shape
        row_block = inv_factor.shape[0]
        features = feat_block * feats_n
        row, feat = lax.axis_index("row"), lax.axis_index("feat")
        rows = rows_dev * rows_n

        small = jnp.stack([weights, strata.astype(jnp.float32)])
        small_all = lax.all_gather(small, "row", axis=1, tiled=True)
        weights_all, strata_all = small_all[0], small_all[1].astype(jnp.int32)

        chunks = {}
        held = candidates
        for k in range(hi_n):
            if k:
                held = send(held, hi_pairs)
            chunks[k, 0] = held
            other = held
            for s in range(1, lo_n):
                other = send(other, lo_pairs)
                chunks[k, s] = other

        groups = [[(0, s) for s in range(lo_n)] + [(1, 0)]]
        for k in range(1, hi_n):
            groups.append([(k, s) for s in range(1, lo_n)] + ([(k + 1, 0)] if k + 1 < hi_n else []))

        offset = row % per_feat * row_block
        root_row = row // per_feat
        sums, columns = {}, []
        for group in groups:
            block = jnp.concatenate([chunks[slot] for slot in group], axis=0)
            part = lax.dot_general(
                block, inv_factor, (((1,), (1,)), ((), ())), preferred_element_type=jnp.float32
            )
            width = row_block
            bit = 1
            while bit < feats_n:
                width //= 2
                mine_high = (feat // bit) % 2
                keep = lax.dynamic_slice_in_dim(part, mine_high * width, width, 1)
                away = lax.dynamic_slice_in_dim(part, (1 - mine_high) * width, width, 1)
                got = send(away.astype(jnp.bfloat16), perm(lambda r, f: (r, f ^ bit)))
                part = keep + got.astype(jnp.float32)
                bit *= 2
            square = jnp.sum(part * part, axis=1).reshape(len(group), rows_dev)
            for i, slot in enumerate(group):
                sums[slot] = square[i]

            mine = lax.dynamic_slice_in_dim(block, offset, row_block, 1)
            value = jnp.where(feat == root_row, mine, jnp.zeros_like(mine))
            half = mine.shape[0] // 2
            low, high = value[:half], value[half:]
            beside = send(value, perm(lambda r, f: (r, f ^ 1), lambda r, f: f == root(r)))
            bit = 2
            while bit < feats_n:
                def held_by(r, f, core):
                    d = f ^ root(r)
                    return d == 0 or (1 < d < bit and (d & 1) == core)
                low = low + send(low, [
                    (r * feats_n + f, r * feats_n + (f ^ bit))
                    for r, f in pairs_row if held_by(r, f, 0)
                ])
                high = high + send(high, [
                    (r * feats_n + f, r * feats_n + (f ^ bit ^ (1 if f == root(r) else 0)))
                    for r, f in pairs_row if held_by(r, f, 1)
                ])
                bit *= 2
            far = ((feat ^ root_row) // 2) != 0
            swap = perm(lambda r, f: (r, f ^ 1), lambda r, f: (f ^ root(r)) > 1)
            is_low = ((feat ^ root_row) & 1) == 0
            other = send(jnp.where(is_low, low, high), swap)
            far_value = jnp.concatenate(
                [jnp.where(is_low, low, other), jnp.where(is_low, other, high)], axis=0
            )
            columns.append(jnp.where(far, far_value, value + beside))

        order = [slot for group in groups for slot in group]
        table = jnp.asarray(
            [[source_table[r][slots.index(slot)] for slot in order] for r in range(rows_n)], jnp.int32
        )
        places = table[row]
        one_hot = (places[None, :] == jnp.arange(rows_n, dtype=jnp.int32)[:, None]).astype(jnp.float32)
        local = jnp.stack([sums[slot] for slot in order])
        total = jnp.sum(one_hot[:, :, None] * local[None, :, :], axis=1)

        def exchange(x, axis_n, first, count, on_row):
            got = [x]
            for d in range(1, count):
                if on_row:
                    pairs = perm(lambda r, f: (r ^ (d * first), f))
                else:
                    pairs = perm(lambda r, f: (r, f ^ (d * first)))
                got.append(send(x, pairs))
            return tree_sum(got)

        total = exchange(total, feats_n, 1, feats_n, False)
        first = 1
        while first < rows_n:
            count = min(8, rows_n // first)
            total = exchange(total, rows_n, first, count, True)
            first *= count

        raw_all = total.reshape(rows)
        strata_count = 2 * rows_n
        membership = (
            strata_all[:, None] == jnp.arange(strata_count, dtype=jnp.int32)[None, :]
        ).astype(jnp.float32)
        products = weights_all * raw_all
        stratum_product = jnp.sum(membership * products[:, None], axis=0)
        stratum_mass = jnp.sum(membership * weights_all[:, None], axis=0)
        stratum_ratio = stratum_mass / stratum_product
        row_ratio = jnp.sum(
            jnp.where(membership > 0, stratum_ratio[None, :], 0.0), axis=1
        )
        new_all = products * row_ratio
        step = (new_all - weights_all).reshape(rows_n, rows_dev)
        step_local = jnp.sum(one_hot[:, :, None] * step[:, None, :], axis=0).reshape(rows)

        gathered = jnp.concatenate([chunks[slot] for slot in order], axis=0)
        column_block = jnp.concatenate(columns, axis=0)
        scaled = (step_local[:, None] * gathered.astype(jnp.float32)).astype(jnp.bfloat16)
        information = lax.dot_general(
            column_block, scaled, (((0,), (0,)), ((), ())), preferred_element_type=jnp.float32
        )
        new_weight = lax.dynamic_slice_in_dim(new_all, row * rows_dev, rows_dev)
        leverage = lax.dynamic_slice_in_dim(raw_all, row * rows_dev, rows_dev) / features
        return (new_weight, leverage, information)

    return per_device


def solution(mesh):
    in_specs = (P("row", "feat"), P("row", "feat"), P("row"), P("row"))
    out_specs = (P("row"), P("row"), P("row", "feat"))
    return jax.shard_map(
        make(mesh), mesh=mesh, in_specs=in_specs, out_specs=out_specs, check_vma=False
    )
```

```python
import functools

import jax
import jax.numpy as jnp
from jax import lax
from jax.experimental import pallas as pl
from jax.experimental.pallas import tpu as pltpu
from jax.sharding import PartitionSpec as P

BOTH = ("row", "feat")
HI = 4
CUTS = 2
MIB = 1 << 20


def ring_order(count):
    return list(range(0, count, 2)) + list(range(1, count, 2))[::-1]


def ring_next(count):
    order = ring_order(count)
    return {order[i]: order[(i + 1) % count] for i in range(count)}


def whiten_kernel(half, cut, order_ref, f_ref, *refs):
    pieces, (keep_ref, away_ref, x_ref) = refs[:-3], refs[-3:]
    step = pl.program_id(0)

    @pl.when(step == 0)
    def _():
        for i, piece in enumerate(pieces):
            x_ref[pl.ds(i * cut, cut), :] = piece[...]

    part = lax.dot_general(
        f_ref[...], x_ref[...], (((1,), (1,)), ((), ())), preferred_element_type=jnp.float32
    )

    @pl.when(step < half)
    def _():
        keep_ref[...] = part

    @pl.when(step >= half)
    def _():
        away_ref[...] = part.astype(jnp.bfloat16)


def whiten(inv_factor, pieces, order, tile):
    row_block, feat_block = inv_factor.shape
    cut = pieces[0].shape[0]
    rows = cut * len(pieces)
    steps = row_block // tile
    half = steps // 2
    grid_spec = pltpu.PrefetchScalarGridSpec(
        num_scalar_prefetch=1,
        grid=(steps,),
        in_specs=[pl.BlockSpec((tile, feat_block), lambda i, order: (order[i], 0))]
        + [pl.BlockSpec((cut, feat_block), lambda i, order: (0, 0))] * len(pieces),
        out_specs=[
            pl.BlockSpec((tile, rows), lambda i, order: (jnp.minimum(i, half - 1), 0)),
            pl.BlockSpec((tile, rows), lambda i, order: (jnp.maximum(i - half, 0), 0)),
        ],
        scratch_shapes=[pltpu.VMEM((rows, feat_block), jnp.bfloat16)],
    )
    return pl.pallas_call(
        functools.partial(whiten_kernel, half, cut),
        grid_spec=grid_spec,
        out_shape=[
            jax.ShapeDtypeStruct((row_block // 2, rows), jnp.float32),
            jax.ShapeDtypeStruct((row_block // 2, rows), jnp.bfloat16),
        ],
        compiler_params=pltpu.CompilerParams(
            dimension_semantics=("arbitrary",), vmem_limit_bytes=24 * MIB
        ),
        cost_estimate=pl.CostEstimate(flops=1000, bytes_accessed=1000, transcendentals=0),
        name="whiten",
    )(order, inv_factor, *pieces)


def information_kernel(cut, d_ref, col_ref, *refs):
    pieces, (out_ref, s_ref) = refs[:-2], refs[-2:]
    lanes = d_ref.shape[1]
    for i, piece in enumerate(pieces):
        scale = d_ref[pl.ds(i * cut, cut), :]
        for c in range(piece.shape[1] // lanes):
            value = piece[:, c * lanes:(c + 1) * lanes].astype(jnp.float32)
            s_ref[pl.ds(i * cut, cut), c * lanes:(c + 1) * lanes] = (scale * value).astype(jnp.bfloat16)
    out_ref[...] = lax.dot_general(
        col_ref[...], s_ref[...], (((1,), (0,)), ((), ())), preferred_element_type=jnp.float32
    )


def increment(step_wide, column_t, pieces, width):
    rows, lanes = step_wide.shape
    row_block = column_t.shape[0]
    cut, feat_block = pieces[0].shape
    return pl.pallas_call(
        functools.partial(information_kernel, cut),
        grid=(feat_block // width,),
        in_specs=[
            pl.BlockSpec((rows, lanes), lambda j: (0, 0)),
            pl.BlockSpec((row_block, rows), lambda j: (0, 0)),
        ]
        + [pl.BlockSpec((cut, width), lambda j: (0, j))] * len(pieces),
        out_specs=pl.BlockSpec((row_block, width), lambda j: (0, j)),
        out_shape=jax.ShapeDtypeStruct((row_block, feat_block), jnp.float32),
        scratch_shapes=[pltpu.VMEM((rows, width), jnp.bfloat16)],
        compiler_params=pltpu.CompilerParams(
            dimension_semantics=("arbitrary",), vmem_limit_bytes=32 * MIB
        ),
        name="increment",
    )(step_wide, column_t, *pieces)


def make(mesh):
    rows_n, feats_n = mesh.shape["row"], mesh.shape["feat"]
    hi_n = HI
    lo_n = rows_n // hi_n
    per_feat = rows_n // feats_n
    everyone = [(r, f) for r in range(rows_n) for f in range(feats_n)]

    def perm(target, keep=lambda r, f: True):
        out = []
        for r, f in everyone:
            if keep(r, f):
                r2, f2 = target(r, f)
                out.append((r * feats_n + f, r2 * feats_n + f2))
        return out

    def send(x, pairs):
        return lax.ppermute(x, BOTH, pairs)

    hi_next, lo_next = ring_next(hi_n), ring_next(lo_n)
    hi_pairs = perm(lambda r, f: (hi_next[r // lo_n] * lo_n + r % lo_n, f))
    lo_pairs = perm(lambda r, f: (r // lo_n * lo_n + lo_next[r % lo_n], f))
    hi_order, lo_order = ring_order(hi_n), ring_order(lo_n)

    def source(r, k, s):
        h, l = r // lo_n, r % lo_n
        h2 = hi_order[(hi_order.index(h) - k) % hi_n]
        l2 = lo_order[(lo_order.index(l) - s) % lo_n]
        return h2 * lo_n + l2

    feat_bits = [1 << b for b in range(feats_n.bit_length() - 1)]
    row_bits = [1 << b for b in range(rows_n.bit_length() - 1)]
    relative = [0]
    for bit in reversed(feat_bits):
        relative = relative + [j + bit for j in relative]

    def per_device(candidates, inv_factor, weights, strata):
        rows_dev, feat_block = candidates.shape
        row_block = inv_factor.shape[0]
        features = feat_block * feats_n
        rows = rows_dev * rows_n
        row, feat = lax.axis_index("row"), lax.axis_index("feat")
        row_numbers = jnp.arange(rows_n, dtype=jnp.int32)
        cut = rows_dev // CUTS

        chunks = {}
        for h in range(CUTS):
            held = candidates[h * cut:(h + 1) * cut]
            for k in range(hi_n):
                if k:
                    held = send(held, hi_pairs)
                chunks[k, 0, h] = other = held
                for s in range(1, lo_n):
                    chunks[k, s, h] = other = send(other, lo_pairs)

        small = jnp.stack([weights, strata.astype(jnp.float32)])
        small_all = jnp.where((row_numbers == row)[:, None, None], small[None], 0.0)
        for bit in row_bits:
            small_all = small_all + send(small_all, perm(lambda r, f: (r ^ bit, f)))
        weights_all = small_all[:, 0].reshape(rows)
        strata_all = small_all[:, 1].reshape(rows).astype(jnp.int32)

        groups = [
            [(k, s) for k in ks for s in range(lo_n)] for ks in [[0, 1]] + [[k] for k in range(2, hi_n)]
        ]
        order = [slot for group in groups for slot in group]
        offset = row % per_feat * row_block
        apart = feat ^ (row // per_feat)
        tile = min(256, row_block // feats_n)
        per_block = row_block // feats_n // tile
        tiles = (
            (jnp.asarray(relative, jnp.int32) ^ feat)[:, None] * per_block
            + jnp.arange(per_block, dtype=jnp.int32)[None, :]
        ).reshape(-1)

        sums, columns = [], []
        for group in groups:
            pieces = [chunks[k, s, h] for k, s in group for h in range(CUTS)]
            mine = jnp.concatenate(
                [lax.dynamic_slice_in_dim(p, offset, row_block, 1) for p in pieces], axis=0
            )
            for bit in feat_bits:
                got = send(mine, perm(
                    lambda r, f: (r, f ^ bit), lambda r, f: (f ^ (r // per_feat)) < bit
                ))
                mine = jnp.where(apart < bit, mine, got)
            columns.append(mine)

            part, away = whiten(inv_factor, pieces, tiles, tile)
            for bit in feat_bits:
                got = send(away, perm(lambda r, f: (r, f ^ bit)))
                part = part + got.astype(jnp.float32)
                if bit != feat_bits[-1]:
                    left = part.shape[0] // 2
                    away = part[left:].astype(jnp.bfloat16)
                    part = part[:left]
            sums.append(jnp.sum(part * part, axis=0))

        table = jnp.asarray([[source(r, *slot) for slot in order] for r in range(rows_n)], jnp.int32)
        places = table[row]
        one_hot = (places[None, :] == row_numbers[:, None]).astype(jnp.float32)
        local = jnp.concatenate(sums).reshape(rows_n, rows_dev)
        total = jnp.sum(one_hot[:, :, None] * local[None, :, :], axis=1)
        for bit in feat_bits:
            total = total + send(total, perm(lambda r, f: (r, f ^ bit)))
        for bit in row_bits:
            total = total + send(total, perm(lambda r, f: (r ^ bit, f)))

        raw_all = total.reshape(rows)
        strata_count = 2 * rows_n
        member = strata_all[:, None] == jnp.arange(strata_count, dtype=jnp.int32)[None, :]
        products = weights_all * raw_all
        stratum_product = jnp.sum(jnp.where(member, products[:, None], 0.0), axis=0)
        stratum_mass = jnp.sum(jnp.where(member, weights_all[:, None], 0.0), axis=0)
        stratum_ratio = stratum_mass / stratum_product
        row_ratio = jnp.sum(jnp.where(member, stratum_ratio[None, :], 0.0), axis=1)
        new_all = products * row_ratio
        step = (new_all - weights_all).reshape(rows_n, rows_dev)
        step_local = jnp.sum(one_hot[:, :, None] * step[:, None, :], axis=0).reshape(rows)
        step_wide = jnp.broadcast_to(step_local[:, None], (rows, 128))

        pieces = [chunks[k, s, h] for k, s in order for h in range(CUTS)]
        column_t = jnp.concatenate(columns, axis=0).T
        information = increment(step_wide, column_t, pieces, min(512, feat_block))
        new_weight = lax.dynamic_slice_in_dim(new_all, row * rows_dev, rows_dev)
        leverage = lax.dynamic_slice_in_dim(raw_all, row * rows_dev, rows_dev) / features
        return (new_weight, leverage, information)

    return per_device


def solution(mesh):
    in_specs = (P("row", "feat"), P("row", "feat"), P("row"), P("row"))
    out_specs = (P("row"), P("row"), P("row", "feat"))
    return jax.shard_map(
        make(mesh), mesh=mesh, in_specs=in_specs, out_specs=out_specs, check_vma=False
    )
```

```python
import functools

import jax
import jax.numpy as jnp
from jax import lax
from jax.experimental import pallas as pl
from jax.experimental.pallas import tpu as pltpu
from jax.sharding import PartitionSpec as P

BOTH = ("row", "feat")
HI = 4
CUTS = 2
MIB = 1 << 20


def ring_order(count):
    return list(range(0, count, 2)) + list(range(1, count, 2))[::-1]


def ring_next(count):
    order = ring_order(count)
    return {order[i]: order[(i + 1) % count] for i in range(count)}


def whiten_kernel(cut, places_ref, f_ref, *refs):
    pieces, (keep_ref, away_ref, mine_ref, x_ref, xt_ref) = refs[:-5], refs[-5:]
    for i, piece in enumerate(pieces):
        x_ref[pl.ds(i * cut, cut), :] = piece[...]
    rows, features = x_ref.shape
    wide = min(512, features)
    for c in range(features // wide):
        xt_ref[pl.ds(c * wide, wide), :] = x_ref[:, c * wide:(c + 1) * wide].T
    steps = places_ref.shape[0] - 1
    half = keep_ref.shape[0]
    tile = 2 * half // steps

    def tile_of(i):
        start = pl.multiple_of(places_ref[i], tile)
        return jnp.dot(f_ref[pl.ds(start, tile), :], xt_ref[...], preferred_element_type=jnp.float32)

    def away(i, carry):
        place = pl.multiple_of(i * tile, tile)
        away_ref[pl.ds(place, tile), :] = tile_of(steps // 2 + i).astype(jnp.bfloat16)
        return carry

    def keep(i, carry):
        keep_ref[pl.ds(pl.multiple_of(i * tile, tile), tile), :] = tile_of(i)
        return carry

    lax.fori_loop(0, steps // 2, away, 0)
    lax.fori_loop(0, steps // 2, keep, 0)
    start = pl.multiple_of(places_ref[steps], mine_ref.shape[0])
    mine_ref[...] = xt_ref[pl.ds(start, mine_ref.shape[0]), :]


def whiten(inv_factor, pieces, places):
    row_block, feat_block = inv_factor.shape
    cut = pieces[0].shape[0]
    rows = cut * len(pieces)
    whole = pl.BlockSpec(memory_space=pltpu.VMEM)
    return pl.pallas_call(
        functools.partial(whiten_kernel, cut),
        in_specs=[pl.BlockSpec(memory_space=pltpu.SMEM)] + [whole] * (1 + len(pieces)),
        out_specs=[whole] * 3,
        out_shape=[
            jax.ShapeDtypeStruct((row_block // 2, rows), jnp.float32),
            jax.ShapeDtypeStruct((row_block // 2, rows), jnp.bfloat16),
            jax.ShapeDtypeStruct((row_block, rows), jnp.bfloat16),
        ],
        scratch_shapes=[
            pltpu.VMEM((rows, feat_block), jnp.bfloat16),
            pltpu.VMEM((feat_block, rows), jnp.bfloat16),
        ],
        compiler_params=pltpu.CompilerParams(vmem_limit_bytes=24 * MIB),
        cost_estimate=pl.CostEstimate(flops=1000, bytes_accessed=1000, transcendentals=0),
        name="whiten",
    )(places, inv_factor, *pieces)


def weight_kernel(strata_n, features, row_ref, raw_ref, w_ref, strata_ref, wide_ref, new_ref, lev_ref, all_ref):
    raw, weights, strata = raw_ref[...], w_ref[...], strata_ref[...]
    products = weights * raw
    ratio = jnp.zeros_like(raw)
    for s in range(strata_n):
        inside = strata == float(s)
        mass = jnp.sum(jnp.where(inside, weights, 0.0), keepdims=True)
        product = jnp.sum(jnp.where(inside, products, 0.0), keepdims=True)
        ratio = jnp.where(inside, mass / product, ratio)
    new = products * ratio
    all_ref[...] = new
    new_ref[...] = all_ref[pl.ds(row_ref[0], 1), :]
    lev_ref[...] = raw_ref[pl.ds(row_ref[0], 1), :] / features
    step = new - weights
    groups, count = step.shape
    for g in range(groups):
        wide_ref[pl.ds(g * count, count), :] = jnp.broadcast_to(step[g:g + 1, :], (128, count)).T


def weight_step(row, raw, weights, strata, features):
    groups, count = raw.shape
    whole = pl.BlockSpec(memory_space=pltpu.VMEM)
    return pl.pallas_call(
        functools.partial(weight_kernel, 2 * groups, features),
        in_specs=[pl.BlockSpec(memory_space=pltpu.SMEM)] + [whole] * 3,
        out_specs=[whole] * 3,
        out_shape=[
            jax.ShapeDtypeStruct((groups * count, 128), jnp.float32),
            jax.ShapeDtypeStruct((1, count), jnp.float32),
            jax.ShapeDtypeStruct((1, count), jnp.float32),
        ],
        scratch_shapes=[pltpu.VMEM((groups, count), jnp.float32)],
        name="weight_step",
    )(row, raw, weights, strata)


def information_kernel(cut, per_slot, groups, steps, starts_ref, d_ref, *refs):
    columns, pieces = refs[:groups], refs[groups:-4]
    out_ref, col_ref, even_ref, odd_ref = refs[-4:]
    j = pl.program_id(0)
    lanes = d_ref.shape[1]

    def scale_into(s_ref):
        for i, piece in enumerate(pieces):
            start = pl.multiple_of(starts_ref[i // per_slot] + i % per_slot * cut, cut)
            scale = d_ref[pl.ds(start, cut), :]
            for c in range(piece.shape[1] // lanes):
                value = piece[:, c * lanes:(c + 1) * lanes].astype(jnp.float32)
                s_ref[pl.ds(i * cut, cut), c * lanes:(c + 1) * lanes] = (scale * value).astype(jnp.bfloat16)

    def product(s_ref):
        out_ref[...] = jnp.dot(col_ref[...], s_ref[...], preferred_element_type=jnp.float32)

    @pl.when(j == 0)
    def _():
        place = 0
        for column in columns:
            width = column.shape[1]
            col_ref[:, place:place + width] = column[...]
            place += width
        scale_into(even_ref)

    @pl.when(j % 2 == 1)
    def _():
        scale_into(odd_ref)
        product(even_ref)

    @pl.when((j > 0) & (j % 2 == 0))
    def _():
        scale_into(even_ref)
        product(odd_ref)


def increment(starts, step_wide, columns, pieces, width, per_slot):
    rows, lanes = step_wide.shape
    row_block = columns[0].shape[0]
    cut, feat_block = pieces[0].shape
    steps = feat_block // width
    grid_spec = pltpu.PrefetchScalarGridSpec(
        num_scalar_prefetch=1,
        grid=(steps + 1,),
        in_specs=[pl.BlockSpec((rows, lanes), lambda j, starts: (0, 0))]
        + [pl.BlockSpec(c.shape, lambda j, starts: (0, 0)) for c in columns]
        + [pl.BlockSpec((cut, width), lambda j, starts: (0, jnp.minimum(j, steps - 1)))] * len(pieces),
        out_specs=pl.BlockSpec((row_block, width), lambda j, starts: (0, jnp.maximum(j - 1, 0))),
        scratch_shapes=[pltpu.VMEM((row_block, rows), jnp.bfloat16)]
        + [pltpu.VMEM((rows, width), jnp.bfloat16)] * 2,
    )
    return pl.pallas_call(
        functools.partial(information_kernel, cut, per_slot, len(columns), steps),
        grid_spec=grid_spec,
        out_shape=jax.ShapeDtypeStruct((row_block, feat_block), jnp.float32),
        compiler_params=pltpu.CompilerParams(
            dimension_semantics=("arbitrary",), vmem_limit_bytes=56 * MIB
        ),
        name="increment",
    )(starts, step_wide, *columns, *pieces)


def make(mesh):
    rows_n, feats_n = mesh.shape["row"], mesh.shape["feat"]
    hi_n = HI
    lo_n = rows_n // hi_n
    per_feat = rows_n // feats_n
    everyone = [(r, f) for r in range(rows_n) for f in range(feats_n)]

    def perm(target, keep=lambda r, f: True):
        out = []
        for r, f in everyone:
            if keep(r, f):
                r2, f2 = target(r, f)
                out.append((r * feats_n + f, r2 * feats_n + f2))
        return out

    def send(x, pairs):
        return lax.ppermute(x, BOTH, pairs)

    hi_next, lo_next = ring_next(hi_n), ring_next(lo_n)
    hi_pairs = perm(lambda r, f: (hi_next[r // lo_n] * lo_n + r % lo_n, f))
    lo_pairs = perm(lambda r, f: (r // lo_n * lo_n + lo_next[r % lo_n], f))
    hi_order, lo_order = ring_order(hi_n), ring_order(lo_n)

    def source(r, k, s):
        h, l = r // lo_n, r % lo_n
        h2 = hi_order[(hi_order.index(h) - k) % hi_n]
        l2 = lo_order[(lo_order.index(l) - s) % lo_n]
        return h2 * lo_n + l2

    feat_bits = [1 << b for b in range(feats_n.bit_length() - 1)]
    row_bits = [1 << b for b in range(rows_n.bit_length() - 1)]
    relative = [0]
    for bit in reversed(feat_bits):
        relative = relative + [j + bit for j in relative]

    def per_device(candidates, inv_factor, weights, strata):
        rows_dev, feat_block = candidates.shape
        row_block = inv_factor.shape[0]
        features = feat_block * feats_n
        rows = rows_dev * rows_n
        row, feat = lax.axis_index("row"), lax.axis_index("feat")
        row_numbers = jnp.arange(rows_n, dtype=jnp.int32)
        cut = rows_dev // CUTS

        tile = min(256, row_block // feats_n)
        per_block = row_block // feats_n // tile
        tiles = (
            (jnp.asarray(relative, jnp.int32) ^ feat)[:, None] * per_block
            + jnp.arange(per_block, dtype=jnp.int32)[None, :]
        ).reshape(-1) * tile
        places = jnp.concatenate([tiles, (row % per_feat * row_block)[None]])
        apart = feat ^ (row // per_feat)
        core = feat % 2
        near = apart < 2

        def swap_feat(x, bit, keep=lambda apart: True):
            return send(x, perm(lambda r, f: (r, f ^ bit), lambda r, f: keep(f ^ (r // per_feat))))

        def to_next(xs):
            return [send(x, hi_pairs) for x in xs]

        def to_side(xs):
            return [send(x, lo_pairs) for x in xs]

        def column_near(mine):
            got = swap_feat(mine, 1, lambda apart: apart == 0)
            return jnp.where(apart == 0, mine, got)

        def column_far(mine):
            half = row_block // 2
            part = lax.dynamic_slice_in_dim(mine, core * half, half, 0)
            for bit in feat_bits[1:]:
                got = swap_feat(part, bit, lambda apart: apart < bit)
                part = jnp.where(apart < bit, part, got)
            return part

        def column_join(mine, part):
            got = swap_feat(part, 1, lambda apart: apart > 1)
            low = jnp.where(core == 0, part, got)
            high = jnp.where(core == 0, got, part)
            return jnp.where(near, mine, jnp.concatenate([low, high], axis=0))

        def reduce_near(keep, away):
            part = keep + swap_feat(away, 1).astype(jnp.float32)
            return part

        def reduce_far(part):
            for bit in feat_bits[1:]:
                left = part.shape[0] // 2
                got = swap_feat(part[left:].astype(jnp.bfloat16), bit)
                part = part[:left] + got.astype(jnp.float32)
            return jnp.sum(part * part, axis=0)

        fence = lax.optimization_barrier
        own = [candidates[h * cut:(h + 1) * cut] for h in range(CUTS)]

        def around(xs):
            rows_of = [xs]
            for _ in range(1, lo_n):
                rows_of.append(to_side(rows_of[-1]))
            return rows_of

        small = jnp.stack([weights, strata.astype(jnp.float32)])
        small_all = jnp.where((row_numbers == row)[:, None, None], small[None], 0.0)
        next_held = to_next(own)
        here = around(own)
        for bit in row_bits:
            small_all = small_all + send(small_all, perm(lambda r, f: (r ^ bit, f)))
        next_held, here, small_all = fence((next_held, here, small_all))
        arrived, swapped, near_parts, sums, mines, halves = [here], [], [], [], [], []
        for k in range(1, hi_n):
            last = k == hi_n - 1
            held = next_held
            slot = arrived[-1]
            if last:
                around_k = [held]
                before = slot
                for s in range(1, lo_n):
                    side = send(around_k[-1][0], lo_pairs)
                    along = send(before[s][1], hi_pairs)
                    around_k.append([side, along])
                here = around_k
            else:
                next_held = to_next(held)
                here = around(held)
            keep, away, mine = whiten(inv_factor, [p for xs in slot for p in xs], places)
            near_part = reduce_near(keep, away)
            mine = column_near(mine)
            if near_parts:
                total_part = reduce_far(near_parts[-1])
                sums.append(total_part)
                far_half = column_far(mines[-1])
                if last:
                    next_held, here, near_part, mine, sums = fence((next_held, here, near_part, mine, sums))
                else:
                    next_held, here, near_part, mine, sums, far_half = fence(
                        (next_held, here, near_part, mine, sums, far_half)
                    )
                halves.append(far_half)
            else:
                next_held, here, near_part, mine = fence((next_held, here, near_part, mine))
            near_parts.append(near_part)
            mines.append(mine)
            arrived.append(here)

        keep, away, mine = whiten(inv_factor, [p for xs in arrived[-1] for p in xs], places)
        near_part = reduce_near(keep, away)
        sums.append(reduce_far(near_parts[-1]))
        near_part, sums, halves = fence((near_part, sums, halves))
        sums.append(reduce_far(near_part))
        mine = column_near(mine)
        sums, mine = fence((sums, mine))
        mines.append(mine)
        while len(halves) < len(mines):
            halves.append(column_far(mines[len(halves)]))

        order = [(k, s) for k in range(hi_n) for s in range(lo_n)]
        table = jnp.asarray([[source(r, *slot) for slot in order] for r in range(rows_n)], jnp.int32)
        sources = table[row]
        one_hot = (sources[None, :] == row_numbers[:, None]).astype(jnp.float32)
        local = jnp.concatenate(sums).reshape(rows_n, rows_dev)
        total = jnp.sum(one_hot[:, :, None] * local[None, :, :], axis=1)
        total = total + swap_feat(total, 1)
        for bit in row_bits:
            total = total + send(total, perm(lambda r, f: (r ^ bit, f)))
        total, halves = fence((total, halves))
        for bit in feat_bits[1:]:
            total = total + swap_feat(total, bit)
        columns = [column_join(*pair) for pair in zip(mines, halves)]
        step_wide, new_weight, leverage = weight_step(
            row[None], total, small_all[:, 0], small_all[:, 1], features
        )
        pieces = [p for slot in arrived for xs in slot for p in xs]
        information = increment(
            sources * rows_dev, step_wide, columns, pieces, min(512, feat_block), CUTS
        )
        return (new_weight.reshape(rows_dev), leverage.reshape(rows_dev), information)

    return per_device


def solution(mesh):
    in_specs = (P("row", "feat"), P("row", "feat"), P("row"), P("row"))
    out_specs = (P("row"), P("row"), P("row", "feat"))
    return jax.shard_map(
        make(mesh), mesh=mesh, in_specs=in_specs, out_specs=out_specs, check_vma=False
    )
```

```python
import functools

import jax
import jax.numpy as jnp
from jax import lax
from jax.experimental import pallas as pl
from jax.experimental.pallas import tpu as pltpu
from jax.sharding import PartitionSpec as P

BOTH = ("row", "feat")
HI = 4
MIB = 1 << 20
LANES = 128


def ring_order(count):
    return list(range(0, count, 2)) + list(range(1, count, 2))[::-1]


def ring_next(count):
    order = ring_order(count)
    return {order[i]: order[(i + 1) % count] for i in range(count)}


def call(kernel, name, grid, in_specs, out_specs, out_shape, scratch, vmem=24):
    return pl.pallas_call(
        kernel,
        grid_spec=pltpu.PrefetchScalarGridSpec(
            num_scalar_prefetch=1,
            grid=grid,
            in_specs=in_specs,
            out_specs=out_specs,
            scratch_shapes=scratch,
        ),
        out_shape=out_shape,
        compiler_params=pltpu.CompilerParams(
            dimension_semantics=("arbitrary",) * len(grid), vmem_limit_bytes=vmem * MIB
        ),
        cost_estimate=pl.CostEstimate(flops=1000, bytes_accessed=1000, transcendentals=0),
        name=name,
    )


def whole(shape):
    return pl.BlockSpec(shape, lambda i, s: (0,) * len(shape))


def whiten_kernel(steps, fold, starts_ref, f_ref, *refs):
    pieces, (keep_ref, away_ref, x_ref, sum_ref) = refs[:-4], refs[-4:]
    step = pl.program_id(0)
    place = 0
    for piece in pieces:
        x_ref[pl.ds(place, piece.shape[0]), :] = piece[...]
        place += piece.shape[0]
    part = jnp.dot(f_ref[...], x_ref[...].T, preferred_element_type=jnp.float32)

    @pl.when(step == 0)
    def _():
        sum_ref[...] = part

    @pl.when(step > 0)
    def _():
        sum_ref[...] += part

    @pl.when(step == steps - 1)
    def _():
        blocks = starts_ref.shape[0]
        size = sum_ref.shape[0] // blocks
        short = size // fold
        for i in range(blocks):
            start = pl.multiple_of(starts_ref[i], size)
            block = jnp.concatenate(
                [sum_ref[pl.ds(start + j * short, short), :] for j in range(fold)], axis=1
            )
            if i < blocks // 2:
                keep_ref[pl.ds(i * short, short), :] = block
            else:
                away_ref[pl.ds((i - blocks // 2) * short, short), :] = block.astype(jnp.bfloat16)


def whiten(starts, inv_factor, pieces):
    row_block, feat_block = inv_factor.shape
    rows = sum(p.shape[0] for p in pieces)
    fold = max(1, LANES // rows)
    width = min(512, feat_block)
    steps = feat_block // width
    out = (row_block // 2 // fold, rows * fold)
    return call(
        functools.partial(whiten_kernel, steps, fold),
        "whiten",
        (steps,),
        [pl.BlockSpec((row_block, width), lambda i, s: (0, i))]
        + [pl.BlockSpec((p.shape[0], width), lambda i, s: (0, i)) for p in pieces],
        [whole(out)] * 2,
        [jax.ShapeDtypeStruct(out, jnp.float32), jax.ShapeDtypeStruct(out, jnp.bfloat16)],
        [pltpu.VMEM((rows, width), jnp.bfloat16), pltpu.VMEM((row_block, rows), jnp.float32)],
        vmem=50,
    )(starts, inv_factor, *pieces)


def pick_kernel(_, *refs):
    place = 0
    for piece in refs[:-1]:
        refs[-1][pl.ds(place, piece.shape[0]), :] = piece[...]
        place += piece.shape[0]


def pick(block, pieces, width):
    rows = sum(p.shape[0] for p in pieces)
    return call(
        pick_kernel,
        "pick",
        (1,),
        [pl.BlockSpec((p.shape[0], width), lambda i, s: (0, s[0])) for p in pieces],
        whole((rows, width)),
        jax.ShapeDtypeStruct((rows, width), jnp.bfloat16),
        [],
    )(block, *pieces)


def pack_kernel(count, flags_ref, *refs):
    out_ref = refs[-1]

    def copy(sources):
        place = 0
        for source in sources:
            out_ref[pl.ds(place, source.shape[0]), :] = source[...]
            place += source.shape[0]

    @pl.when(flags_ref[0] == 1)
    def _():
        copy(refs[:count])

    @pl.when(flags_ref[0] == 0)
    def _():
        copy(refs[count:-1])


def pack(flag, own, got):
    rows, width = sum(x.shape[0] for x in own), own[0].shape[1]
    return call(
        functools.partial(pack_kernel, len(own)),
        "pack",
        (1,),
        [whole(x.shape) for x in own + got],
        whole((rows, width)),
        jax.ShapeDtypeStruct((rows, width), jnp.bfloat16),
        [],
    )(flag, *own, *got)


def join_kernel(flags_ref, own_ref, other_ref, out_ref):
    wide = min(256, own_ref.shape[1])

    def turn(source):
        for c in range(source.shape[1] // wide):
            out_ref[pl.ds(c * wide, wide), :] = source[:, c * wide:(c + 1) * wide].T

    @pl.when(flags_ref[0] == 1)
    def _():
        turn(own_ref)

    @pl.when(flags_ref[0] == 0)
    def _():
        turn(other_ref)


def join(flag, own, other):
    rows, width = own.shape
    return call(
        join_kernel,
        "join",
        (1,),
        [whole(own.shape)] * 2,
        whole((width, rows)),
        jax.ShapeDtypeStruct((width, rows), jnp.bfloat16),
        [],
    )(flag, own, other)


def square_kernel(sizes, places_ref, *refs):
    out_ref = refs[-1]
    count = out_ref.shape[1]
    slot = 0
    for g, size in enumerate(sizes):
        value = refs[2 * g][...] + refs[2 * g + 1][...].astype(jnp.float32)
        line = jnp.sum(value * value, axis=0, keepdims=True)
        for i in range(size):
            total = line[:, i * count:(i + 1) * count]
            for j in range(1, line.shape[1] // (size * count)):
                total += line[:, (j * size + i) * count:(j * size + i + 1) * count]
            out_ref[pl.ds(places_ref[slot], 1), :] = total
            slot += 1


def squares(places, pairs, sizes, count):
    shapes = [x.shape for pair in pairs for x in pair]
    out = (sum(sizes), count)
    return call(
        functools.partial(square_kernel, sizes),
        "squares",
        (1,),
        [whole(shape) for shape in shapes],
        whole(out),
        jax.ShapeDtypeStruct(out, jnp.float32),
        [],
    )(places, *[x for pair in pairs for x in pair])


def weight_kernel(strata_n, features, row_ref, raw_ref, w_ref, strata_ref, wide_ref, new_ref, lev_ref, all_ref):
    raw, weights, strata = raw_ref[...], w_ref[...], strata_ref[...]
    products = weights * raw
    ratio = jnp.zeros_like(raw)
    for s in range(strata_n):
        inside = strata == float(s)
        mass = jnp.sum(jnp.where(inside, weights, 0.0), keepdims=True)
        product = jnp.sum(jnp.where(inside, products, 0.0), keepdims=True)
        ratio = jnp.where(inside, mass / product, ratio)
    new = products * ratio
    all_ref[...] = new
    new_ref[...] = all_ref[pl.ds(row_ref[0], 1), :]
    lev_ref[...] = raw_ref[pl.ds(row_ref[0], 1), :] / features
    step = new - weights
    groups, count = step.shape
    for g in range(groups):
        wide_ref[pl.ds(g * count, count), :] = jnp.broadcast_to(step[g:g + 1, :], (LANES, count)).T


def weight_step(row, raw, weights, strata, features):
    groups, count = raw.shape
    return call(
        functools.partial(weight_kernel, 2 * groups, features),
        "weight_step",
        (1,),
        [whole(raw.shape)] * 3,
        [whole((groups * count, LANES)), whole((1, count)), whole((1, count))],
        [
            jax.ShapeDtypeStruct((groups * count, LANES), jnp.float32),
            jax.ShapeDtypeStruct((1, count), jnp.float32),
            jax.ShapeDtypeStruct((1, count), jnp.float32),
        ],
        [pltpu.VMEM((groups, count), jnp.float32)],
    )(row, raw, weights, strata)


def information_kernel(starts_ref, d_ref, col_ref, *refs):
    pieces, (out_ref, s_ref) = refs[:-2], refs[-2:]
    place = 0
    for i, piece in enumerate(pieces):
        size = piece.shape[0]
        scale = d_ref[pl.ds(pl.multiple_of(starts_ref[i], size), size), :]
        for c in range(piece.shape[1] // LANES):
            value = piece[:, c * LANES:(c + 1) * LANES].astype(jnp.float32)
            s_ref[pl.ds(place, size), c * LANES:(c + 1) * LANES] = (scale * value).astype(jnp.bfloat16)
        place += size
    out_ref[...] = jnp.dot(col_ref[...], s_ref[...], preferred_element_type=jnp.float32)


def increment(starts, step_wide, column_t, pieces):
    row_block, rows = column_t.shape
    feat_block = pieces[0].shape[1]
    width = min(512, feat_block)
    return call(
        information_kernel,
        "increment",
        (feat_block // width,),
        [whole(step_wide.shape), whole(column_t.shape)]
        + [pl.BlockSpec((p.shape[0], width), lambda i, s: (0, i)) for p in pieces],
        pl.BlockSpec((row_block, width), lambda i, s: (0, i)),
        jax.ShapeDtypeStruct((row_block, feat_block), jnp.float32),
        [pltpu.VMEM((rows, width), jnp.bfloat16)],
        vmem=44,
    )(starts, step_wide, column_t, *pieces)


def make(mesh):
    rows_n, feats_n = mesh.shape["row"], mesh.shape["feat"]
    hi_n = HI
    lo_n = rows_n // hi_n
    per_feat = rows_n // feats_n
    everyone = [(r, f) for r in range(rows_n) for f in range(feats_n)]

    def perm(target, keep=lambda r, f: True):
        out = []
        for r, f in everyone:
            if keep(r, f):
                r2, f2 = target(r, f)
                out.append((r * feats_n + f, r2 * feats_n + f2))
        return out

    def send(x, pairs):
        return lax.ppermute(x, BOTH, pairs)

    def swap(x, r_bit, f_bit):
        return send(x, perm(lambda r, f: (r ^ r_bit, f ^ f_bit)))

    fence = lax.optimization_barrier
    hi_next, lo_next = ring_next(hi_n), ring_next(lo_n)
    hi_pairs = perm(lambda r, f: (hi_next[r // lo_n] * lo_n + r % lo_n, f))
    lo_pairs = perm(lambda r, f: (r // lo_n * lo_n + lo_next[r % lo_n], f))
    hi_order, lo_order = ring_order(hi_n), ring_order(lo_n)

    def source(r, k, s):
        h, l = r // lo_n, r % lo_n
        h2 = hi_order[(hi_order.index(h) - k) % hi_n]
        l2 = lo_order[(lo_order.index(l) - s) % lo_n]
        return h2 * lo_n + l2

    feat_bits = [1 << b for b in range(feats_n.bit_length() - 1)]
    far_bits = feat_bits[1:]
    row_bits = [1 << b for b in range(rows_n.bit_length() - 1)]
    relative = [0]
    for bit in reversed(feat_bits):
        relative = relative + [j + bit for j in relative]

    groups = [[(0, s) for s in range(lo_n)] + [(1, 0)]]
    for k in range(1, hi_n):
        groups.append([(k, s) for s in range(1, lo_n)] + ([(k + 1, 0)] if k + 1 < hi_n else []))
    slots = [slot for group in groups for slot in group]

    def per_device(candidates, inv_factor, weights, strata):
        rows_dev, feat_block = candidates.shape
        row_block = inv_factor.shape[0]
        features = feat_block * feats_n
        half = rows_dev // 2
        row, feat = lax.axis_index("row"), lax.axis_index("feat")
        starts = (jnp.asarray(relative, jnp.int32) ^ feat) * (row_block // feats_n)
        table = jnp.asarray([[source(r, *slot) for slot in slots] for r in range(rows_n)], jnp.int32)
        places = table[row]
        block = (row % per_feat)[None]
        apart = feat ^ (row // per_feat)

        def pieces_of(chosen):
            return [p for slot in chosen for p in chunks[slot]]

        def column_far(mine):
            for bit in reversed(far_bits):
                got = send(mine, perm(
                    lambda r, f: (r, f ^ bit),
                    lambda r, f: (f ^ (r // per_feat)) % (2 * bit) == 0,
                ))
                if len(far_bits) > 1:
                    mine = got = jnp.where(apart % (2 * bit) == 0, mine, got)
            return got

        def halve(part, got):
            part = part + got.astype(jnp.float32)
            left = part.shape[0] // 2
            return part[:left], part[left:].astype(jnp.bfloat16)

        chunks = {(0, 0): [candidates]}
        small = jnp.stack([weights, strata.astype(jnp.float32)])
        small_all = jnp.where((jnp.arange(rows_n) == row)[:, None, None], small[None], 0.0)
        small_bits = list(row_bits)

        columns, far_columns, near, far = [], [], {}, {}
        for k in range(hi_n + 1):
            fresh, out = [], {}
            if k < hi_n - 1:
                fresh.append((k + 1, 0))
                chunks[k + 1, 0] = [send(chunks[k, 0][0], hi_pairs)]
            if k < hi_n:
                held = chunks[k, 0][0]
                for s in range(1, lo_n):
                    fresh.append((k, s))
                    if k < hi_n - 1:
                        held = send(held, lo_pairs)
                        chunks[k, s] = [held]
                    else:
                        held = send(held[:half], lo_pairs)
                        chunks[k, s] = [held, send(chunks[k - 1, s][0][half:], hi_pairs)]
            out["fresh"] = [chunks[slot] for slot in fresh]
            if small_bits:
                bit = small_bits.pop(0)
                out["small"] = small_all + swap(small_all, bit, 0)
            if k > 0:
                group = pieces_of(groups[k - 1])
                mine = pick(block, group, row_block)
                columns.append(mine)
                out["far_column"] = column_far(mine)
                out["white"] = whiten(starts, inv_factor, group)
            if k > 1:
                keep, away = near[k - 2]
                out["near"] = halve(keep, swap(away, 0, 1))
            if k > 2:
                keep, away = far[k - 3]
                for bit in far_bits[:-1]:
                    keep, away = halve(keep, swap(away, 0, bit))
                out["far"] = (keep, swap(away, 0, far_bits[-1]))
            out = fence(out)
            for slot, value in zip(fresh, out["fresh"]):
                chunks[slot] = value
            small_all = out.get("small", small_all)
            if k > 0:
                far_columns.append(out["far_column"])
                near[k - 1] = out["white"]
            if k > 1:
                far[k - 2] = out["near"]
            if k > 2:
                far[k - 3] = out["far"]
        while small_bits:
            small_all = small_all + swap(small_all, small_bits.pop(0), 0)

        def last_far(g):
            keep, away = far[g]
            for bit in far_bits[:-1]:
                keep, away = halve(keep, swap(away, 0, bit))
            return keep, swap(away, 0, far_bits[-1])

        keep, away = near[hi_n - 1]
        far[hi_n - 1] = fence(halve(keep, swap(away, 0, 1)))
        packed = pack((apart == 0).astype(jnp.int32)[None], columns, far_columns)
        far[hi_n - 2], far[hi_n - 1], packed = fence((last_far(hi_n - 2), last_far(hi_n - 1), packed))
        total = squares(places, [far[g] for g in range(hi_n)], [len(g) for g in groups], rows_dev)

        total = total + swap(total, 0, 1)
        bits = [(0, bit) for bit in far_bits] + [(bit, 0) for bit in row_bits]
        beside = swap(packed, 0, 1)
        column_t = None
        while bits:
            first, rest = bits[0], bits[1:2]
            bits = bits[2:]
            if rest:
                second = rest[0]
                both = (first[0] ^ second[0], first[1] ^ second[1])
                total = (total + swap(total, *first)) + (swap(total, *second) + swap(total, *both))
            else:
                total = total + swap(total, *first)
            if beside is not None:
                total, beside = fence((total, beside))
                column_t = join((apart % 2 == 0).astype(jnp.int32)[None], packed, beside)
                beside = None
            elif column_t is not None and bits:
                total, column_t = fence((total, column_t))
        total, column_t = fence((total, column_t))

        step_wide, new_weight, leverage = weight_step(
            row[None], total, small_all[:, 0], small_all[:, 1], features
        )
        piece_starts = []
        for i, slot in enumerate(slots):
            place = places[i] * rows_dev
            for piece in chunks[slot]:
                piece_starts.append(place)
                place = place + piece.shape[0]
        information = increment(jnp.stack(piece_starts), step_wide, column_t, pieces_of(slots))
        return (new_weight.reshape(rows_dev), leverage.reshape(rows_dev), information)

    return per_device


def solution(mesh):
    in_specs = (P("row", "feat"), P("row", "feat"), P("row"), P("row"))
    out_specs = (P("row"), P("row"), P("row", "feat"))
    return jax.shard_map(
        make(mesh), mesh=mesh, in_specs=in_specs, out_specs=out_specs, check_vma=False
    )
```

```python
import functools

import jax
import jax.numpy as jnp
from jax import lax
from jax.experimental import pallas as pl
from jax.experimental.pallas import tpu as pltpu
from jax.sharding import PartitionSpec as P

BOTH = ("row", "feat")
HI = 4
MIB = 1 << 20
LANES = 128


def ring_order(count):
    return list(range(0, count, 2)) + list(range(1, count, 2))[::-1]


def ring_next(count):
    order = ring_order(count)
    return {order[i]: order[(i + 1) % count] for i in range(count)}


def call(kernel, name, out_shape, scratch, args, fixed=(), vmem=16, flops=1000):
    on_vmem = pl.BlockSpec(memory_space=pltpu.VMEM)
    on_hbm = pl.BlockSpec(memory_space=pltpu.HBM)
    scalars, rest = args
    out_hbm = "out" in fixed
    held = [x for x in fixed if not isinstance(x, str)]
    return pl.pallas_call(
        kernel,
        in_specs=[pl.BlockSpec(memory_space=pltpu.SMEM)] + [on_hbm] * len(held) + [on_vmem] * len(rest),
        out_specs=jax.tree.map(lambda _: on_hbm if out_hbm else on_vmem, out_shape),
        out_shape=out_shape,
        scratch_shapes=scratch,
        compiler_params=pltpu.CompilerParams(vmem_limit_bytes=vmem * MIB),
        cost_estimate=pl.CostEstimate(flops=flops, bytes_accessed=1000, transcendentals=0),
        name=name,
    )(scalars, *held, *rest)


def whiten_kernel(tile, starts_ref, f_ref, *refs):
    pieces, (keep_ref, away_ref, x_ref, xt_ref, buf_ref, sems) = refs[:-6], refs[-6:]
    slots = buf_ref.shape[0]
    tiles = f_ref.shape[0] // tile
    per_block = tiles // starts_ref.shape[0]
    half = tiles // 2

    def copy(t):
        order = lax.rem(t + half, tiles)
        start = starts_ref[order // per_block] + lax.rem(order, per_block) * tile
        slot = lax.rem(t, slots)
        return pltpu.make_async_copy(
            f_ref.at[pl.ds(pl.multiple_of(start, tile), tile)], buf_ref.at[slot], sems.at[slot]
        )

    for t in range(min(slots, tiles)):
        copy(jnp.int32(t)).start()
    place = 0
    for piece in pieces:
        x_ref[pl.ds(place, piece.shape[0]), :] = piece[...]
        place += piece.shape[0]
    wide = min(512, x_ref.shape[1])
    for c in range(x_ref.shape[1] // wide):
        xt_ref[pl.ds(c * wide, wide), :] = x_ref[:, c * wide:(c + 1) * wide].T

    def product(t):
        copy(t).wait()
        part = jnp.dot(buf_ref[lax.rem(t, slots)], xt_ref[...], preferred_element_type=jnp.float32)

        @pl.when(t + slots < tiles)
        def _():
            copy(t + slots).start()

        return part

    def away(t, carry):
        away_ref[pl.ds(pl.multiple_of(t * tile, tile), tile), :] = product(t).astype(jnp.bfloat16)
        return carry

    def keep(t, carry):
        keep_ref[pl.ds(pl.multiple_of((t - half) * tile, tile), tile), :] = product(t)
        return carry

    lax.fori_loop(0, half, away, 0)
    lax.fori_loop(half, tiles, keep, 0)


def whiten(starts, inv_factor, pieces):
    row_block, feat_block = inv_factor.shape
    rows = sum(p.shape[0] for p in pieces)
    tile = min(256, row_block // starts.shape[0])
    slots = 3
    out = (row_block // 2, rows)
    return call(
        functools.partial(whiten_kernel, tile),
        "whiten",
        [jax.ShapeDtypeStruct(out, jnp.float32), jax.ShapeDtypeStruct(out, jnp.bfloat16)],
        [
            pltpu.VMEM((rows, feat_block), jnp.bfloat16),
            pltpu.VMEM((feat_block, rows), jnp.bfloat16),
            pltpu.VMEM((slots, tile, feat_block), jnp.bfloat16),
            pltpu.SemaphoreType.DMA((slots,)),
        ],
        (starts, pieces),
        (inv_factor,),
        vmem=46,
        flops=8 * row_block * feat_block * rows,
    )


def halve_kernel(_, part_ref, got_ref, keep_ref, away_ref):
    left = keep_ref.shape[0]
    keep_ref[...] = part_ref[:left, :] + got_ref[:left, :].astype(jnp.float32)
    away_ref[...] = (part_ref[left:, :] + got_ref[left:, :].astype(jnp.float32)).astype(jnp.bfloat16)


def halve(starts, part, got):
    out = (part.shape[0] // 2, part.shape[1])
    return call(
        halve_kernel,
        "halve",
        [jax.ShapeDtypeStruct(out, jnp.float32), jax.ShapeDtypeStruct(out, jnp.bfloat16)],
        [],
        (starts, [part, got]),
    )


def pick_kernel(count, half, block_ref, *refs):
    pieces, outs = refs[:count], refs[count:]
    width = outs[0].shape[1]
    start = pl.multiple_of(block_ref[0] * width, width)
    place = 0
    for piece in pieces:
        outs[0][pl.ds(place, piece.shape[0]), :] = piece[:, pl.ds(start, width)]
        place += piece.shape[0]
    if half:
        outs[1][...] = pieces[-1][:half, :]
        for out, piece in zip(outs[2:], pieces):
            out[...] = piece[half:, :]


def pick(block, pieces, width, half=0):
    rows = sum(p.shape[0] for p in pieces)
    out = [jax.ShapeDtypeStruct((rows, width), jnp.bfloat16)]
    if half:
        out += [jax.ShapeDtypeStruct((half, pieces[0].shape[1]), jnp.bfloat16)] * len(pieces)
    return call(
        functools.partial(pick_kernel, len(pieces), half), "pick", out, [], (block, pieces)
    )


def pack_kernel(count, flag_ref, *refs):
    out_ref = refs[-1]

    def copy(sources):
        place = 0
        for source in sources:
            out_ref[pl.ds(place, source.shape[0]), :] = source[...]
            place += source.shape[0]

    @pl.when(flag_ref[0] == 1)
    def _():
        copy(refs[:count])

    @pl.when(flag_ref[0] == 0)
    def _():
        copy(refs[count:-1])


def pack(flag, own, got):
    out = (sum(x.shape[0] for x in own), own[0].shape[1])
    return call(
        functools.partial(pack_kernel, len(own)),
        "pack",
        jax.ShapeDtypeStruct(out, jnp.bfloat16),
        [],
        (flag, own + got),
    )


def join_kernel(flag_ref, own_ref, other_ref, out_ref):
    wide = min(256, own_ref.shape[1])

    def turn(source):
        for c in range(source.shape[1] // wide):
            out_ref[pl.ds(c * wide, wide), :] = source[:, c * wide:(c + 1) * wide].T

    @pl.when(flag_ref[0] == 1)
    def _():
        turn(own_ref)

    @pl.when(flag_ref[0] == 0)
    def _():
        turn(other_ref)


def join(flag, own, other):
    rows, width = own.shape
    return call(
        join_kernel, "join", jax.ShapeDtypeStruct((width, rows), jnp.bfloat16), [], (flag, [own, other])
    )


def square_kernel(sizes, places_ref, *refs):
    out_ref = refs[-1]
    count = out_ref.shape[1]
    slot = 0
    for g, size in enumerate(sizes):
        value = refs[2 * g][...] + refs[2 * g + 1][...].astype(jnp.float32)
        line = jnp.sum(value * value, axis=0, keepdims=True)
        for i in range(size):
            out_ref[pl.ds(places_ref[slot], 1), :] = line[:, i * count:(i + 1) * count]
            slot += 1


def squares(places, pairs, sizes, count):
    return call(
        functools.partial(square_kernel, sizes),
        "squares",
        jax.ShapeDtypeStruct((sum(sizes), count), jnp.float32),
        [],
        (places, [x for pair in pairs for x in pair]),
    )


def weight_kernel(strata_n, features, row_ref, raw_ref, w_ref, strata_ref, wide_ref, new_ref, lev_ref, all_ref):
    raw, weights, strata = raw_ref[...], w_ref[...], strata_ref[...]
    products = weights * raw
    ratio = jnp.zeros_like(raw)
    for s in range(strata_n):
        inside = strata == float(s)
        mass = jnp.sum(jnp.where(inside, weights, 0.0), keepdims=True)
        product = jnp.sum(jnp.where(inside, products, 0.0), keepdims=True)
        ratio = jnp.where(inside, mass / product, ratio)
    new = products * ratio
    all_ref[...] = new
    new_ref[...] = all_ref[pl.ds(row_ref[0], 1), :]
    lev_ref[...] = raw_ref[pl.ds(row_ref[0], 1), :] / features
    step = new - weights
    groups, count = step.shape
    for g in range(groups):
        wide_ref[pl.ds(g * count, count), :] = jnp.broadcast_to(step[g:g + 1, :], (LANES, count)).T


def weight_step(row, raw, weights, strata, features):
    groups, count = raw.shape
    return call(
        functools.partial(weight_kernel, 2 * groups, features),
        "weight_step",
        [
            jax.ShapeDtypeStruct((groups * count, LANES), jnp.float32),
            jax.ShapeDtypeStruct((1, count), jnp.float32),
            jax.ShapeDtypeStruct((1, count), jnp.float32),
        ],
        [pltpu.VMEM((groups, count), jnp.float32)],
        (row, [raw, weights, strata]),
    )


def information_kernel(starts_ref, d_ref, col_ref, *refs):
    pieces, (out_ref, s_ref, buf_ref, sems) = refs[:-4], refs[-4:]
    width = s_ref.shape[1]
    steps = out_ref.shape[1] // width

    def copy(j):
        slot = lax.rem(j, 2)
        return pltpu.make_async_copy(
            buf_ref.at[slot], out_ref.at[:, pl.ds(pl.multiple_of(j * width, width), width)], sems.at[slot]
        )

    def step(j, carry):
        place = 0
        for i, piece in enumerate(pieces):
            size = piece.shape[0]
            scale = d_ref[pl.ds(pl.multiple_of(starts_ref[i], size), size), :]
            for c in range(width // LANES):
                start = pl.multiple_of(j * width + c * LANES, LANES)
                value = piece[:, pl.ds(start, LANES)].astype(jnp.float32)
                s_ref[pl.ds(place, size), c * LANES:(c + 1) * LANES] = (scale * value).astype(jnp.bfloat16)
            place += size

        @pl.when(j > 1)
        def _():
            copy(j - 2).wait()

        buf_ref[lax.rem(j, 2)] = jnp.dot(col_ref[...], s_ref[...], preferred_element_type=jnp.float32)
        copy(j).start()
        return carry

    lax.fori_loop(0, steps, step, 0)
    for j in range(max(0, steps - 2), steps):
        copy(jnp.int32(j)).wait()


def increment(starts, step_wide, column_t, pieces):
    row_block, rows = column_t.shape
    feat_block = pieces[0].shape[1]
    width = min(512, feat_block)
    return call(
        information_kernel,
        "increment",
        jax.ShapeDtypeStruct((row_block, feat_block), jnp.float32),
        [
            pltpu.VMEM((rows, width), jnp.bfloat16),
            pltpu.VMEM((2, row_block, width), jnp.float32),
            pltpu.SemaphoreType.DMA((2,)),
        ],
        (starts, [step_wide, column_t] + pieces),
        ("out",),
        24,
    )


def make(mesh):
    rows_n, feats_n = mesh.shape["row"], mesh.shape["feat"]
    hi_n = HI
    lo_n = rows_n // hi_n
    per_feat = rows_n // feats_n
    everyone = [(r, f) for r in range(rows_n) for f in range(feats_n)]

    def perm(target, keep=lambda r, f: True):
        out = []
        for r, f in everyone:
            if keep(r, f):
                r2, f2 = target(r, f)
                out.append((r * feats_n + f, r2 * feats_n + f2))
        return out

    def send(x, pairs):
        return lax.ppermute(x, BOTH, pairs)

    def swap(x, r_bit, f_bit):
        return send(x, perm(lambda r, f: (r ^ r_bit, f ^ f_bit)))

    fence = lax.optimization_barrier
    hi_next, lo_next = ring_next(hi_n), ring_next(lo_n)
    hi_pairs = perm(lambda r, f: (hi_next[r // lo_n] * lo_n + r % lo_n, f))
    lo_pairs = perm(lambda r, f: (r // lo_n * lo_n + lo_next[r % lo_n], f))
    hi_order, lo_order = ring_order(hi_n), ring_order(lo_n)

    def source(r, k, s):
        h, l = r // lo_n, r % lo_n
        h2 = hi_order[(hi_order.index(h) - k) % hi_n]
        l2 = lo_order[(lo_order.index(l) - s) % lo_n]
        return h2 * lo_n + l2

    feat_bits = [1 << b for b in range(feats_n.bit_length() - 1)]
    far_bits = feat_bits[1:]
    row_bits = [1 << b for b in range(rows_n.bit_length() - 1)]
    relative = [0]
    for bit in reversed(feat_bits):
        relative = relative + [j + bit for j in relative]

    groups = [[(0, s) for s in range(lo_n)] + [(1, 0)]]
    for k in range(1, hi_n):
        groups.append([(k, s) for s in range(1, lo_n)] + ([(k + 1, 0)] if k + 1 < hi_n else []))
    slots = [slot for group in groups for slot in group]
    white_groups = [[(k, s) for s in range(lo_n)] for k in range(hi_n)]
    white_slots = [slot for group in white_groups for slot in group]

    def per_device(candidates, inv_factor, weights, strata):
        rows_dev, feat_block = candidates.shape
        row_block = inv_factor.shape[0]
        features = feat_block * feats_n
        half = rows_dev // 2
        row, feat = lax.axis_index("row"), lax.axis_index("feat")
        starts = (jnp.asarray(relative, jnp.int32) ^ feat) * (row_block // feats_n)
        def sources(chosen):
            table = [[source(r, *slot) for slot in chosen] for r in range(rows_n)]
            return jnp.asarray(table, jnp.int32)[row]

        places, white_places = sources(slots), sources(white_slots)
        block = (row % per_feat)[None]
        apart = feat ^ (row // per_feat)

        def pieces_of(chosen):
            return [p for slot in chosen for p in chunks[slot]]

        def column_far(mine):
            for bit in reversed(far_bits):
                got = send(mine, perm(
                    lambda r, f: (r, f ^ bit),
                    lambda r, f: (f ^ (r // per_feat)) % (2 * bit) == 0,
                ))
                if len(far_bits) > 1:
                    mine = got = jnp.where(apart % (2 * bit) == 0, mine, got)
            return got

        def to_far(near):
            keep, away = halve(starts, *near)
            for bit in far_bits[:-1]:
                keep, away = halve(starts, keep, swap(away, 0, bit))
            return keep, swap(away, 0, far_bits[-1])

        chunks = {(0, 0): [candidates]}
        small = jnp.stack([weights, strata.astype(jnp.float32)])
        small_all = jnp.where((jnp.arange(rows_n) == row)[:, None, None], small[None], 0.0)
        small_bits = list(row_bits)

        columns, far_columns, white, near, far = [], [], [], [], []
        for k in range(hi_n + 1):
            fresh, out = [], {}
            if k > 0:
                last = k == hi_n - 1
                picked = pick(block, pieces_of(groups[k - 1]), row_block, half if last else 0)
                columns.append(picked[0])
            if k < hi_n - 1:
                fresh.append((k + 1, 0))
                chunks[k + 1, 0] = [send(chunks[k, 0][0], hi_pairs)]
                held = chunks[k, 0][0]
                for s in range(1, lo_n):
                    fresh.append((k, s))
                    held = send(held, lo_pairs)
                    chunks[k, s] = [held]
            elif k < hi_n:
                held = picked[1]
                for s in range(1, lo_n):
                    fresh.append((k, s))
                    held = send(held, lo_pairs)
                    chunks[k, s] = [held, send(picked[1 + s], hi_pairs)]
            out["fresh"] = [chunks[slot] for slot in fresh]
            if small_bits:
                bit = small_bits.pop(0)
                out["small"] = small_all + swap(small_all, bit, 0)
            if k > 0:
                out["column"] = column_far(columns[-1])
                out["white"] = whiten(starts, inv_factor, pieces_of(white_groups[k - 1]))
            if k > 1:
                keep, away = white[k - 2]
                out["near"] = keep, swap(away, 0, 1)
            if k > 2:
                out["far"] = to_far(near[k - 3])
            out = fence(out)
            for slot, value in zip(fresh, out["fresh"]):
                chunks[slot] = value
            small_all = out.get("small", small_all)
            for name, kept in (("column", far_columns), ("white", white), ("near", near), ("far", far)):
                if name in out:
                    kept.append(out[name])
        while small_bits:
            small_all = small_all + swap(small_all, small_bits.pop(0), 0)

        keep, away = white[-1]
        packed = pack((apart == 0).astype(jnp.int32)[None], columns, far_columns)
        last, before, packed = fence(((keep, swap(away, 0, 1)), to_far(near[-1]), packed))
        far.append(before)
        last, beside = fence((to_far(last), swap(packed, 0, 1)))
        far.append(last)
        total = squares(white_places, far, [len(g) for g in white_groups], rows_dev)
        total = fence(total + swap(total, 0, 1))
        column_t = join((apart % 2 == 0).astype(jnp.int32)[None], packed, beside)
        bits = [(0, bit) for bit in far_bits] + [(bit, 0) for bit in row_bits]
        for i, bit in enumerate(bits):
            total = total + swap(total, *bit)
            if i == 0:
                total, column_t = fence((total, column_t))

        step_wide, new_weight, leverage = weight_step(
            row[None], total, small_all[:, 0], small_all[:, 1], features
        )
        piece_starts = []
        for i, slot in enumerate(slots):
            place = places[i] * rows_dev
            for piece in chunks[slot]:
                piece_starts.append(place)
                place = place + piece.shape[0]
        information = increment(jnp.stack(piece_starts), step_wide, column_t, pieces_of(slots))
        return (new_weight.reshape(rows_dev), leverage.reshape(rows_dev), information)

    return per_device


def solution(mesh):
    in_specs = (P("row", "feat"), P("row", "feat"), P("row"), P("row"))
    out_specs = (P("row"), P("row"), P("row", "feat"))
    return jax.shard_map(
        make(mesh), mesh=mesh, in_specs=in_specs, out_specs=out_specs, check_vma=False
    )
```

```python
import functools

import jax
import jax.numpy as jnp
from jax import lax
from jax.experimental import pallas as pl
from jax.experimental.pallas import tpu as pltpu
from jax.sharding import PartitionSpec as P

BOTH = ("row", "feat")
HI = 4
MIB = 1 << 20
LANES = 128


def ring_order(count):
    return list(range(0, count, 2)) + list(range(1, count, 2))[::-1]


def ring_next(count):
    order = ring_order(count)
    return {order[i]: order[(i + 1) % count] for i in range(count)}


def call(kernel, name, out_shape, scratch, args, fixed=(), vmem=16, flops=1000):
    on_vmem = pl.BlockSpec(memory_space=pltpu.VMEM)
    on_hbm = pl.BlockSpec(memory_space=pltpu.HBM)
    scalars, rest = args
    out_hbm = "out" in fixed
    held = [x for x in fixed if not isinstance(x, str)]
    return pl.pallas_call(
        kernel,
        in_specs=[pl.BlockSpec(memory_space=pltpu.SMEM)] + [on_hbm] * len(held) + [on_vmem] * len(rest),
        out_specs=jax.tree.map(lambda _: on_hbm if out_hbm else on_vmem, out_shape),
        out_shape=out_shape,
        scratch_shapes=scratch,
        compiler_params=pltpu.CompilerParams(vmem_limit_bytes=vmem * MIB),
        cost_estimate=pl.CostEstimate(flops=flops, bytes_accessed=1000, transcendentals=0),
        name=name,
    )(scalars, *held, *rest)


def touch_kernel(starts_ref, f_ref, out_ref):
    for i in range(starts_ref.shape[0]):
        out_ref[i] = starts_ref[i]


def touch(starts, inv_factor):
    return pl.pallas_call(
        touch_kernel,
        in_specs=[pl.BlockSpec(memory_space=pltpu.SMEM), pl.BlockSpec(memory_space=pltpu.VMEM)],
        out_specs=pl.BlockSpec(memory_space=pltpu.SMEM),
        out_shape=jax.ShapeDtypeStruct(starts.shape, starts.dtype),
        compiler_params=pltpu.CompilerParams(vmem_limit_bytes=16 * MIB),
        cost_estimate=pl.CostEstimate(flops=1000, bytes_accessed=1000, transcendentals=0),
        name="touch",
    )(starts, inv_factor)


def whiten_kernel(starts_ref, f_ref, *refs):
    pieces, (keep_ref, away_ref, x_ref, xt_ref) = refs[:-4], refs[-4:]
    place = 0
    for piece in pieces:
        x_ref[pl.ds(place, piece.shape[0]), :] = piece[...]
        place += piece.shape[0]
    wide = min(512, x_ref.shape[1])
    for c in range(x_ref.shape[1] // wide):
        xt_ref[pl.ds(c * wide, wide), :] = x_ref[:, c * wide:(c + 1) * wide].T
    blocks = starts_ref.shape[0]
    tile = f_ref.shape[0] // blocks

    def product(t):
        start = pl.multiple_of(starts_ref[t], tile)
        return jnp.dot(f_ref[pl.ds(start, tile), :], xt_ref[...], preferred_element_type=jnp.float32)

    def step(t, carry):
        place = pl.multiple_of(t * tile, tile)
        away_ref[pl.ds(place, tile), :] = product(blocks // 2 + t).astype(jnp.bfloat16)
        keep_ref[pl.ds(place, tile), :] = product(t)
        return carry

    lax.fori_loop(0, blocks // 2, step, 0)


def whiten(starts, inv_factor, pieces):
    row_block, feat_block = inv_factor.shape
    rows = sum(p.shape[0] for p in pieces)
    out = (row_block // 2, rows)
    return call(
        whiten_kernel,
        "whiten",
        [jax.ShapeDtypeStruct(out, jnp.float32), jax.ShapeDtypeStruct(out, jnp.bfloat16)],
        [pltpu.VMEM((rows, feat_block), jnp.bfloat16), pltpu.VMEM((feat_block, rows), jnp.bfloat16)],
        (starts, [inv_factor] + pieces),
        flops=8 * row_block * feat_block * rows,
    )


def halve_kernel(_, part_ref, got_ref, keep_ref, away_ref):
    left = keep_ref.shape[0]
    keep_ref[...] = part_ref[:left, :] + got_ref[:left, :].astype(jnp.float32)
    away_ref[...] = (part_ref[left:, :] + got_ref[left:, :].astype(jnp.float32)).astype(jnp.bfloat16)


def halve(starts, part, got):
    out = (part.shape[0] // 2, part.shape[1])
    return call(
        halve_kernel,
        "halve",
        [jax.ShapeDtypeStruct(out, jnp.float32), jax.ShapeDtypeStruct(out, jnp.bfloat16)],
        [],
        (starts, [part, got]),
    )


def pick_kernel(count, half, block_ref, *refs):
    pieces, outs = refs[:count], refs[count:]
    width = outs[0].shape[1]
    start = pl.multiple_of(block_ref[0] * width, width)
    place = 0
    for piece in pieces:
        outs[0][pl.ds(place, piece.shape[0]), :] = piece[:, pl.ds(start, width)]
        place += piece.shape[0]
    if half:
        outs[1][...] = pieces[-1][:half, :]
        for out, piece in zip(outs[2:], pieces):
            out[...] = piece[half:, :]


def pick(block, pieces, width, half=0):
    rows = sum(p.shape[0] for p in pieces)
    out = [jax.ShapeDtypeStruct((rows, width), jnp.bfloat16)]
    if half:
        out += [jax.ShapeDtypeStruct((half, pieces[0].shape[1]), jnp.bfloat16)] * len(pieces)
    return call(
        functools.partial(pick_kernel, len(pieces), half), "pick", out, [], (block, pieces)
    )


def pack_kernel(count, flag_ref, *refs):
    out_ref = refs[-1]

    def copy(sources):
        place = 0
        for source in sources:
            out_ref[pl.ds(place, source.shape[0]), :] = source[...]
            place += source.shape[0]

    @pl.when(flag_ref[0] == 1)
    def _():
        copy(refs[:count])

    @pl.when(flag_ref[0] == 0)
    def _():
        copy(refs[count:-1])


def pack(flag, own, got):
    out = (sum(x.shape[0] for x in own), own[0].shape[1])
    return call(
        functools.partial(pack_kernel, len(own)),
        "pack",
        jax.ShapeDtypeStruct(out, jnp.bfloat16),
        [],
        (flag, own + got),
    )


def join_kernel(flag_ref, own_ref, other_ref, out_ref):
    wide = min(256, own_ref.shape[1])

    def turn(source):
        for c in range(source.shape[1] // wide):
            out_ref[pl.ds(c * wide, wide), :] = source[:, c * wide:(c + 1) * wide].T

    @pl.when(flag_ref[0] == 1)
    def _():
        turn(own_ref)

    @pl.when(flag_ref[0] == 0)
    def _():
        turn(other_ref)


def join(flag, own, other):
    rows, width = own.shape
    return call(
        join_kernel, "join", jax.ShapeDtypeStruct((width, rows), jnp.bfloat16), [], (flag, [own, other])
    )


def square_kernel(sizes, places_ref, w_ref, strata_ref, *refs):
    out_ref = refs[-1]
    count = out_ref.shape[1]
    slots = sum(sizes)
    out_ref[...] = jnp.zeros_like(out_ref)
    slot = 0
    for g, size in enumerate(sizes):
        value = refs[2 * g][...] + refs[2 * g + 1][...].astype(jnp.float32)
        line = jnp.sum(value * value, axis=0, keepdims=True)
        for i in range(size):
            out_ref[pl.ds(places_ref[slot], 1), :] = line[:, i * count:(i + 1) * count]
            slot += 1

    @pl.when(places_ref[slots + 1] == 0)
    def _():
        out_ref[pl.ds(slots + places_ref[slots], 1), :] = w_ref[...]
        out_ref[pl.ds(2 * slots + places_ref[slots], 1), :] = strata_ref[...].astype(jnp.float32)


def squares(places, weights, strata, pairs, sizes):
    count = weights.shape[1]
    return call(
        functools.partial(square_kernel, sizes),
        "squares",
        jax.ShapeDtypeStruct((3 * sum(sizes), count), jnp.float32),
        [],
        (places, [weights, strata] + [x for pair in pairs for x in pair]),
    )


def weight_kernel(strata_n, features, row_ref, sums_ref, wide_ref, new_ref, lev_ref, all_ref):
    groups = sums_ref.shape[0] // 3
    raw, weights, strata = [sums_ref[pl.ds(i * groups, groups), :] for i in range(3)]
    products = weights * raw
    ratio = jnp.zeros_like(raw)
    for s in range(strata_n):
        inside = strata == float(s)
        mass = jnp.sum(jnp.where(inside, weights, 0.0), keepdims=True)
        product = jnp.sum(jnp.where(inside, products, 0.0), keepdims=True)
        ratio = jnp.where(inside, mass / product, ratio)
    new = products * ratio
    all_ref[...] = new
    new_ref[...] = all_ref[pl.ds(row_ref[0], 1), :]
    lev_ref[...] = sums_ref[pl.ds(row_ref[0], 1), :] / features
    step = new - weights
    count = step.shape[1]
    for g in range(groups):
        wide_ref[pl.ds(g * count, count), :] = jnp.broadcast_to(step[g:g + 1, :], (LANES, count)).T


def weight_step(row, sums, features):
    groups, count = sums.shape[0] // 3, sums.shape[1]
    return call(
        functools.partial(weight_kernel, 2 * groups, features),
        "weight_step",
        [
            jax.ShapeDtypeStruct((groups * count, LANES), jnp.float32),
            jax.ShapeDtypeStruct((1, count), jnp.float32),
            jax.ShapeDtypeStruct((1, count), jnp.float32),
        ],
        [pltpu.VMEM((groups, count), jnp.float32)],
        (row, [sums]),
    )


def information_kernel(starts_ref, d_ref, col_ref, *refs):
    pieces, (out_ref, s_ref, buf_ref, sems) = refs[:-4], refs[-4:]
    width = s_ref.shape[1]
    steps = out_ref.shape[1] // width

    def copy(j):
        slot = lax.rem(j, 2)
        return pltpu.make_async_copy(
            buf_ref.at[slot], out_ref.at[:, pl.ds(pl.multiple_of(j * width, width), width)], sems.at[slot]
        )

    def step(j, carry):
        place = 0
        for i, piece in enumerate(pieces):
            size = piece.shape[0]
            scale = d_ref[pl.ds(pl.multiple_of(starts_ref[i], size), size), :]
            for c in range(width // LANES):
                start = pl.multiple_of(j * width + c * LANES, LANES)
                value = piece[:, pl.ds(start, LANES)].astype(jnp.float32)
                s_ref[pl.ds(place, size), c * LANES:(c + 1) * LANES] = (scale * value).astype(jnp.bfloat16)
            place += size

        @pl.when(j > 1)
        def _():
            copy(j - 2).wait()

        buf_ref[lax.rem(j, 2)] = jnp.dot(col_ref[...], s_ref[...], preferred_element_type=jnp.float32)
        copy(j).start()
        return carry

    lax.fori_loop(0, steps, step, 0)
    for j in range(max(0, steps - 2), steps):
        copy(jnp.int32(j)).wait()


def increment(starts, step_wide, column_t, pieces):
    row_block, rows = column_t.shape
    feat_block = pieces[0].shape[1]
    width = min(512, feat_block)
    return call(
        information_kernel,
        "increment",
        jax.ShapeDtypeStruct((row_block, feat_block), jnp.float32),
        [
            pltpu.VMEM((rows, width), jnp.bfloat16),
            pltpu.VMEM((2, row_block, width), jnp.float32),
            pltpu.SemaphoreType.DMA((2,)),
        ],
        (starts, [step_wide, column_t] + pieces),
        ("out",),
        24,
    )


def make(mesh):
    rows_n, feats_n = mesh.shape["row"], mesh.shape["feat"]
    hi_n = HI
    lo_n = rows_n // hi_n
    per_feat = rows_n // feats_n
    everyone = [(r, f) for r in range(rows_n) for f in range(feats_n)]

    def perm(target, keep=lambda r, f: True):
        out = []
        for r, f in everyone:
            if keep(r, f):
                r2, f2 = target(r, f)
                out.append((r * feats_n + f, r2 * feats_n + f2))
        return out

    def send(x, pairs):
        return lax.ppermute(x, BOTH, pairs)

    def swap(x, r_bit, f_bit):
        return send(x, perm(lambda r, f: (r ^ r_bit, f ^ f_bit)))

    fence = lax.optimization_barrier
    hi_next, lo_next = ring_next(hi_n), ring_next(lo_n)
    hi_pairs = perm(lambda r, f: (hi_next[r // lo_n] * lo_n + r % lo_n, f))
    lo_pairs = perm(lambda r, f: (r // lo_n * lo_n + lo_next[r % lo_n], f))
    hi_order, lo_order = ring_order(hi_n), ring_order(lo_n)

    def source(r, k, s):
        h, l = r // lo_n, r % lo_n
        h2 = hi_order[(hi_order.index(h) - k) % hi_n]
        l2 = lo_order[(lo_order.index(l) - s) % lo_n]
        return h2 * lo_n + l2

    feat_bits = [1 << b for b in range(feats_n.bit_length() - 1)]
    far_bits = feat_bits[1:]
    row_bits = [1 << b for b in range(rows_n.bit_length() - 1)]
    relative = [0]
    for bit in reversed(feat_bits):
        relative = relative + [j + bit for j in relative]

    groups = [[(0, s) for s in range(lo_n)] + [(1, 0)]]
    for k in range(1, hi_n):
        groups.append([(k, s) for s in range(1, lo_n)] + ([(k + 1, 0)] if k + 1 < hi_n else []))
    slots = [slot for group in groups for slot in group]
    white_groups = [[(k, s) for s in range(lo_n)] for k in range(hi_n)]
    white_slots = [slot for group in white_groups for slot in group]

    def per_device(candidates, inv_factor, weights, strata):
        rows_dev, feat_block = candidates.shape
        row_block = inv_factor.shape[0]
        features = feat_block * feats_n
        half = rows_dev // 2
        row, feat = lax.axis_index("row"), lax.axis_index("feat")
        starts = (jnp.asarray(relative, jnp.int32) ^ feat) * (row_block // feats_n)
        def sources(chosen):
            table = [[source(r, *slot) for slot in chosen] for r in range(rows_n)]
            return jnp.asarray(table, jnp.int32)[row]

        places, white_places = sources(slots), sources(white_slots)
        block = (row % per_feat)[None]
        apart = feat ^ (row // per_feat)

        def pieces_of(chosen):
            return [p for slot in chosen for p in chunks[slot]]

        def column_far(mine):
            for bit in reversed(far_bits):
                got = send(mine, perm(
                    lambda r, f: (r, f ^ bit),
                    lambda r, f: (f ^ (r // per_feat)) % (2 * bit) == 0,
                ))
                if len(far_bits) > 1:
                    mine = got = jnp.where(apart % (2 * bit) == 0, mine, got)
            return got

        def to_far(near):
            keep, away = halve(starts, *near)
            for bit in far_bits[:-1]:
                keep, away = halve(starts, keep, swap(away, 0, bit))
            return keep, swap(away, 0, far_bits[-1])

        chunks = {(0, 0): [candidates]}
        columns, far_columns, white, near, far = [], [], [], [], []
        for k in range(hi_n + 1):
            fresh, out = [], {}
            if k > 0:
                last = k == hi_n - 1
                picked = pick(block, pieces_of(groups[k - 1]), row_block, half if last else 0)
                columns.append(picked[0])
            if k < hi_n - 1:
                fresh.append((k + 1, 0))
                chunks[k + 1, 0] = [send(chunks[k, 0][0], hi_pairs)]
                held = chunks[k, 0][0]
                for s in range(1, lo_n):
                    fresh.append((k, s))
                    held = send(held, lo_pairs)
                    chunks[k, s] = [held]
            elif k < hi_n:
                held = picked[1]
                for s in range(1, lo_n):
                    fresh.append((k, s))
                    held = send(held, lo_pairs)
                    chunks[k, s] = [held, send(picked[1 + s], hi_pairs)]
            out["fresh"] = [chunks[slot] for slot in fresh]
            if k == 0:
                out["starts"] = touch(starts, inv_factor)
            if k > 0:
                out["column"] = column_far(columns[-1])
                out["white"] = whiten(starts, inv_factor, pieces_of(white_groups[k - 1]))
            if k > 1:
                keep, away = white[k - 2]
                out["near"] = keep, swap(away, 0, 1)
            if k > 2:
                out["far"] = to_far(near[k - 3])
            out = fence(out)
            for slot, value in zip(fresh, out["fresh"]):
                chunks[slot] = value
            starts = out.get("starts", starts)
            for name, kept in (("column", far_columns), ("white", white), ("near", near), ("far", far)):
                if name in out:
                    kept.append(out[name])
        keep, away = white[-1]
        packed = pack((apart == 0).astype(jnp.int32)[None], columns, far_columns)
        last, before, packed = fence(((keep, swap(away, 0, 1)), to_far(near[-1]), packed))
        far.append(before)
        last, beside = fence((to_far(last), swap(packed, 0, 1)))
        far.append(last)
        total = squares(
            jnp.concatenate([white_places, row[None], feat[None]]),
            weights[None],
            strata[None],
            far,
            [len(g) for g in white_groups],
        )
        total = fence(total + swap(total, 0, 1))
        column_t = join((apart % 2 == 0).astype(jnp.int32)[None], packed, beside)
        bits = [(0, bit) for bit in far_bits] + [(bit, 0) for bit in row_bits]
        for i, bit in enumerate(bits):
            total = total + swap(total, *bit)
            if i == 0:
                total, column_t = fence((total, column_t))

        step_wide, new_weight, leverage = weight_step(row[None], total, features)
        piece_starts = []
        for i, slot in enumerate(slots):
            place = places[i] * rows_dev
            for piece in chunks[slot]:
                piece_starts.append(place)
                place = place + piece.shape[0]
        information = increment(jnp.stack(piece_starts), step_wide, column_t, pieces_of(slots))
        return (new_weight.reshape(rows_dev), leverage.reshape(rows_dev), information)

    return per_device


def solution(mesh):
    in_specs = (P("row", "feat"), P("row", "feat"), P("row"), P("row"))
    out_specs = (P("row"), P("row"), P("row", "feat"))
    return jax.shard_map(
        make(mesh), mesh=mesh, in_specs=in_specs, out_specs=out_specs, check_vma=False
    )
```

```python
import functools

import jax
import jax.numpy as jnp
from jax import lax
from jax.experimental import pallas as pl
from jax.experimental.pallas import tpu as pltpu
from jax.sharding import PartitionSpec as P

BOTH = ("row", "feat")
HI = 4
MIB = 1 << 20
LANES = 128
BIG = 56
BLOCK, NEAR, EVEN, ROW, FEAT, STARTS = range(6)


def ring_order(count):
    return list(range(0, count, 2)) + list(range(1, count, 2))[::-1]


def ring_next(count):
    order = ring_order(count)
    return {order[i]: order[(i + 1) % count] for i in range(count)}


def call(kernel, name, out_shape, scratch, args, fixed=(), vmem=16, flops=1000):
    on_vmem = pl.BlockSpec(memory_space=pltpu.VMEM)
    on_hbm = pl.BlockSpec(memory_space=pltpu.HBM)
    scalars, rest = args
    out_hbm = "out" in fixed
    held = [x for x in fixed if not isinstance(x, str)]
    return pl.pallas_call(
        kernel,
        in_specs=[pl.BlockSpec(memory_space=pltpu.SMEM)] + [on_hbm] * len(held) + [on_vmem] * len(rest),
        out_specs=jax.tree.map(lambda _: on_hbm if out_hbm else on_vmem, out_shape),
        out_shape=out_shape,
        scratch_shapes=scratch,
        compiler_params=pltpu.CompilerParams(vmem_limit_bytes=vmem * MIB),
        cost_estimate=pl.CostEstimate(flops=flops, bytes_accessed=1000, transcendentals=0),
        name=name,
    )(scalars, *held, *rest)


def touch_kernel(scalars_ref, f_ref, out_ref):
    for i in range(scalars_ref.shape[0]):
        out_ref[i] = scalars_ref[i]


def touch(scalars, inv_factor):
    return pl.pallas_call(
        touch_kernel,
        in_specs=[pl.BlockSpec(memory_space=pltpu.SMEM), pl.BlockSpec(memory_space=pltpu.VMEM)],
        out_specs=pl.BlockSpec(memory_space=pltpu.SMEM),
        out_shape=jax.ShapeDtypeStruct(scalars.shape, scalars.dtype),
        compiler_params=pltpu.CompilerParams(vmem_limit_bytes=16 * MIB),
        cost_estimate=pl.CostEstimate(flops=1000, bytes_accessed=1000, transcendentals=0),
        name="touch",
    )(scalars, inv_factor)


def whiten_kernel(blocks, scalars_ref, f_ref, *refs):
    pieces, (keep_ref, away_ref, x_ref, xt_ref) = refs[:-4], refs[-4:]
    place = 0
    for piece in pieces:
        x_ref[pl.ds(place, piece.shape[0]), :] = piece[...]
        place += piece.shape[0]
    wide = min(512, x_ref.shape[1])
    for c in range(x_ref.shape[1] // wide):
        xt_ref[pl.ds(c * wide, wide), :] = x_ref[:, c * wide:(c + 1) * wide].T
    tile = f_ref.shape[0] // blocks

    def product(t):
        start = pl.multiple_of(scalars_ref[STARTS + t], tile)
        return jnp.dot(f_ref[pl.ds(start, tile), :], xt_ref[...], preferred_element_type=jnp.float32)

    def step(t, carry):
        place = pl.multiple_of(t * tile, tile)
        away_ref[pl.ds(place, tile), :] = product(blocks // 2 + t).astype(jnp.bfloat16)
        keep_ref[pl.ds(place, tile), :] = product(t)
        return carry

    lax.fori_loop(0, blocks // 2, step, 0)


def whiten(scalars, blocks, inv_factor, pieces):
    row_block, feat_block = inv_factor.shape
    rows = sum(p.shape[0] for p in pieces)
    out = (row_block // 2, rows)
    return call(
        functools.partial(whiten_kernel, blocks),
        "whiten",
        [jax.ShapeDtypeStruct(out, jnp.float32), jax.ShapeDtypeStruct(out, jnp.bfloat16)],
        [pltpu.VMEM((rows, feat_block), jnp.bfloat16), pltpu.VMEM((feat_block, rows), jnp.bfloat16)],
        (scalars, [inv_factor] + pieces),
        flops=8 * row_block * feat_block * rows,
    )


def halve_kernel(_, part_ref, got_ref, keep_ref, away_ref):
    left = keep_ref.shape[0]
    keep_ref[...] = part_ref[:left, :] + got_ref[:left, :].astype(jnp.float32)
    away_ref[...] = (part_ref[left:, :] + got_ref[left:, :].astype(jnp.float32)).astype(jnp.bfloat16)


def halve(scalars, part, got):
    out = (part.shape[0] // 2, part.shape[1])
    return call(
        halve_kernel,
        "halve",
        [jax.ShapeDtypeStruct(out, jnp.float32), jax.ShapeDtypeStruct(out, jnp.bfloat16)],
        [],
        (scalars, [part, got]),
    )


def pick_kernel(count, half, scalars_ref, *refs):
    pieces, outs = refs[:count], refs[count:]
    width = outs[0].shape[1]
    start = pl.multiple_of(scalars_ref[BLOCK] * width, width)
    place = 0
    for piece in pieces:
        outs[0][pl.ds(place, piece.shape[0]), :] = piece[:, pl.ds(start, width)]
        place += piece.shape[0]
    if half:
        outs[1][...] = pieces[-1][:half, :]
        for out, piece in zip(outs[2:], pieces):
            out[...] = piece[half:, :]


def pick(scalars, pieces, width, half=0):
    rows = sum(p.shape[0] for p in pieces)
    out = [jax.ShapeDtypeStruct((rows, width), jnp.bfloat16)]
    if half:
        out += [jax.ShapeDtypeStruct((half, pieces[0].shape[1]), jnp.bfloat16)] * len(pieces)
    return call(
        functools.partial(pick_kernel, len(pieces), half), "pick", out, [], (scalars, pieces)
    )


def fetch(pairs, sems):
    copies = [pltpu.make_async_copy(a, b, sems.at[i]) for i, (a, b) in enumerate(pairs)]
    for copy in copies:
        copy.start()
    return copies


def pack_kernel(count, scalars_ref, *refs):
    out_ref, sems = refs[-2:]

    def copy(sources):
        place, pairs = 0, []
        for source in sources:
            pairs.append((source, out_ref.at[pl.ds(place, source.shape[0])]))
            place += source.shape[0]
        for one in fetch(pairs, sems):
            one.wait()

    @pl.when(scalars_ref[NEAR] == 1)
    def _():
        copy(refs[:count])

    @pl.when(scalars_ref[NEAR] == 0)
    def _():
        copy(refs[count:-2])


def pack(scalars, own, got):
    out = (sum(x.shape[0] for x in own), own[0].shape[1])
    return call(
        functools.partial(pack_kernel, len(own)),
        "pack",
        jax.ShapeDtypeStruct(out, jnp.bfloat16),
        [pltpu.SemaphoreType.DMA((len(own),))],
        (scalars, []),
        tuple(own + got),
        BIG,
    )


def join_kernel(scalars_ref, own_ref, other_ref, out_ref, x_ref, xt_ref, sems):
    @pl.when(scalars_ref[EVEN] == 1)
    def _():
        fetch([(own_ref, x_ref)], sems)[0].wait()

    @pl.when(scalars_ref[EVEN] == 0)
    def _():
        fetch([(other_ref, x_ref)], sems)[0].wait()

    wide = min(256, x_ref.shape[1])
    for c in range(x_ref.shape[1] // wide):
        xt_ref[pl.ds(c * wide, wide), :] = x_ref[:, c * wide:(c + 1) * wide].T
    fetch([(xt_ref, out_ref)], sems)[0].wait()


def join(scalars, own, other):
    rows, width = own.shape
    return call(
        join_kernel,
        "join",
        jax.ShapeDtypeStruct((width, rows), jnp.bfloat16),
        [
            pltpu.VMEM((rows, width), jnp.bfloat16),
            pltpu.VMEM((width, rows), jnp.bfloat16),
            pltpu.SemaphoreType.DMA((1,)),
        ],
        (scalars, []),
        (own, other, "out"),
        BIG,
    )


def square_kernel(sizes, first, scalars_ref, *refs):
    early = 2 * len(sizes) - 2
    held = refs[early + 5:-1]
    w_ref, strata_ref, keep_ref, got_ref, out_ref = refs[early:early + 5]
    copies = fetch(list(zip(refs[:early], held)), refs[-1])
    count = out_ref.shape[1]
    slots = sum(sizes)
    out_ref[...] = jnp.zeros_like(out_ref)

    @pl.when(scalars_ref[FEAT] == 0)
    def _():
        out_ref[pl.ds(slots + scalars_ref[ROW], 1), :] = w_ref[...]
        out_ref[pl.ds(2 * slots + scalars_ref[ROW], 1), :] = strata_ref[...].astype(jnp.float32)

    def put(g, part_ref, other_ref):
        slot = first + sum(sizes[:g])
        value = part_ref[...] + other_ref[...].astype(jnp.float32)
        line = jnp.sum(value * value, axis=0, keepdims=True)
        for i in range(sizes[g]):
            out_ref[pl.ds(scalars_ref[slot + i], 1), :] = line[:, i * count:(i + 1) * count]

    put(len(sizes) - 1, keep_ref, got_ref)
    for copy in copies:
        copy.wait()
    for g in range(len(sizes) - 1):
        put(g, held[2 * g], held[2 * g + 1])


def squares(scalars, first, weights, strata, pairs, sizes):
    count = weights.shape[1]
    early = [x for pair in pairs[:-1] for x in pair]
    return call(
        functools.partial(square_kernel, sizes, first),
        "squares",
        jax.ShapeDtypeStruct((3 * sum(sizes), count), jnp.float32),
        [pltpu.VMEM(x.shape, x.dtype) for x in early] + [pltpu.SemaphoreType.DMA((len(early),))],
        (scalars, [weights, strata] + list(pairs[-1])),
        tuple(early),
        BIG,
    )


def weight_step(strata_n, features, row, sums_ref, new_ref, lev_ref, all_ref, d_ref):
    groups = sums_ref.shape[0] // 3
    raw, weights, strata = [sums_ref[pl.ds(i * groups, groups), :] for i in range(3)]
    products = weights * raw
    ratio = jnp.zeros_like(raw)
    for s in range(strata_n):
        inside = strata == float(s)
        mass = jnp.sum(jnp.where(inside, weights, 0.0), keepdims=True)
        product = jnp.sum(jnp.where(inside, products, 0.0), keepdims=True)
        ratio = jnp.where(inside, mass / product, ratio)
    new = products * ratio
    all_ref[...] = new
    new_ref[...] = all_ref[pl.ds(row, 1), :]
    lev_ref[...] = sums_ref[pl.ds(row, 1), :] / features
    step = new - weights
    count = step.shape[1]
    for g in range(groups):
        d_ref[pl.ds(g * count, count), :] = jnp.broadcast_to(step[g:g + 1, :], (LANES, count)).T


def information_kernel(features, pieces_of, scalars_ref, col_hbm, *refs):
    n = len(pieces_of)
    pieces, sums_ref, out_ref, new_ref, lev_ref = refs[:n], refs[n], *refs[n + 1:n + 4]
    all_ref, d_ref, col_ref, p_ref, s_ref, buf_ref, col_sem, p_sems, sems = refs[n + 4:]
    width = s_ref.shape[1]
    steps = out_ref.shape[1] // width
    count = sums_ref.shape[1]
    sizes = [piece.shape[0] for piece in pieces]
    offsets = [sum(sizes[:i]) for i in range(n)]

    def bring(j, i):
        columns = pl.ds(pl.multiple_of(j * width, width), width)
        return pltpu.make_async_copy(
            pieces[i].at[:, columns], p_ref.at[pl.ds(offsets[i], sizes[i]), columns], p_sems.at[j, i]
        )

    def copy(j):
        slot = lax.rem(j, 2)
        return pltpu.make_async_copy(
            buf_ref.at[slot], out_ref.at[:, pl.ds(pl.multiple_of(j * width, width), width)], sems.at[slot]
        )

    column = pltpu.make_async_copy(col_hbm, col_ref, col_sem.at[0])
    for j in range(steps):
        for i in range(n):
            bring(j, i).start()
        if j == 0:
            column.start()
    weight_step(
        2 * (sums_ref.shape[0] // 3), features, scalars_ref[ROW], sums_ref, new_ref, lev_ref, all_ref, d_ref
    )
    column.wait()

    def step(j, carry):
        for i in range(n):
            bring(j, i).wait()
        for i, (slot, first) in enumerate(pieces_of):
            size = sizes[i]
            start = pl.multiple_of(scalars_ref[slot] * count + first, size)
            scale = d_ref[pl.ds(start, size), :]
            for c in range(width // LANES):
                start = pl.multiple_of(j * width + c * LANES, LANES)
                value = p_ref[pl.ds(offsets[i], size), pl.ds(start, LANES)].astype(jnp.float32)
                s_ref[pl.ds(offsets[i], size), c * LANES:(c + 1) * LANES] = (scale * value).astype(jnp.bfloat16)

        @pl.when(j > 1)
        def _():
            copy(j - 2).wait()

        buf_ref[lax.rem(j, 2)] = jnp.dot(col_ref[...], s_ref[...], preferred_element_type=jnp.float32)
        copy(j).start()
        return carry

    lax.fori_loop(0, steps, step, 0)
    for j in range(max(0, steps - 2), steps):
        copy(jnp.int32(j)).wait()


def increment(scalars, pieces_of, sums, column_t, pieces, features):
    row_block, rows = column_t.shape
    groups, count = sums.shape[0] // 3, sums.shape[1]
    feat_block = pieces[0].shape[1]
    width = min(512, feat_block)
    steps = feat_block // width
    on_vmem = pl.BlockSpec(memory_space=pltpu.VMEM)
    on_hbm = pl.BlockSpec(memory_space=pltpu.HBM)
    return pl.pallas_call(
        functools.partial(information_kernel, features, pieces_of),
        in_specs=[pl.BlockSpec(memory_space=pltpu.SMEM)] + [on_hbm] * (1 + len(pieces)) + [on_vmem],
        out_specs=[on_hbm, on_vmem, on_vmem],
        out_shape=[
            jax.ShapeDtypeStruct((row_block, feat_block), jnp.float32),
            jax.ShapeDtypeStruct((1, count), jnp.float32),
            jax.ShapeDtypeStruct((1, count), jnp.float32),
        ],
        scratch_shapes=[
            pltpu.VMEM((groups, count), jnp.float32),
            pltpu.VMEM((rows, LANES), jnp.float32),
            pltpu.VMEM((row_block, rows), jnp.bfloat16),
            pltpu.VMEM((rows, feat_block), jnp.bfloat16),
            pltpu.VMEM((rows, width), jnp.bfloat16),
            pltpu.VMEM((2, row_block, width), jnp.float32),
            pltpu.SemaphoreType.DMA((1,)),
            pltpu.SemaphoreType.DMA((steps, len(pieces))),
            pltpu.SemaphoreType.DMA((2,)),
        ],
        compiler_params=pltpu.CompilerParams(vmem_limit_bytes=BIG * MIB),
        cost_estimate=pl.CostEstimate(
            flops=2 * row_block * feat_block * rows, bytes_accessed=1000, transcendentals=0
        ),
        name="increment",
    )(scalars, column_t, *pieces, sums)


def make(mesh):
    rows_n, feats_n = mesh.shape["row"], mesh.shape["feat"]
    hi_n = HI
    lo_n = rows_n // hi_n
    per_feat = rows_n // feats_n
    everyone = [(r, f) for r in range(rows_n) for f in range(feats_n)]

    def perm(target, keep=lambda r, f: True):
        out = []
        for r, f in everyone:
            if keep(r, f):
                r2, f2 = target(r, f)
                out.append((r * feats_n + f, r2 * feats_n + f2))
        return out

    def send(x, pairs):
        return lax.ppermute(x, BOTH, pairs)

    def swap(x, r_bit, f_bit):
        return send(x, perm(lambda r, f: (r ^ r_bit, f ^ f_bit)))

    fence = lax.optimization_barrier
    hi_next, lo_next = ring_next(hi_n), ring_next(lo_n)
    hi_pairs = perm(lambda r, f: (hi_next[r // lo_n] * lo_n + r % lo_n, f))
    lo_pairs = perm(lambda r, f: (r // lo_n * lo_n + lo_next[r % lo_n], f))
    hi_order, lo_order = ring_order(hi_n), ring_order(lo_n)

    def source(r, k, s):
        h, l = r // lo_n, r % lo_n
        h2 = hi_order[(hi_order.index(h) - k) % hi_n]
        l2 = lo_order[(lo_order.index(l) - s) % lo_n]
        return h2 * lo_n + l2

    feat_bits = [1 << b for b in range(feats_n.bit_length() - 1)]
    far_bits = feat_bits[1:]
    row_bits = [1 << b for b in range(rows_n.bit_length() - 1)]
    relative = [0]
    for bit in reversed(feat_bits):
        relative = relative + [j + bit for j in relative]

    groups = [[(0, s) for s in range(lo_n)] + [(1, 0)]]
    for k in range(1, hi_n):
        groups.append([(k, s) for s in range(1, lo_n)] + ([(k + 1, 0)] if k + 1 < hi_n else []))
    slots = [slot for group in groups for slot in group]
    white_groups = [[(k, s) for s in range(lo_n)] for k in range(hi_n)]
    white_slots = [slot for group in white_groups for slot in group]

    def per_device(candidates, inv_factor, weights, strata):
        rows_dev, feat_block = candidates.shape
        row_block = inv_factor.shape[0]
        features = feat_block * feats_n
        half = rows_dev // 2
        row, feat = lax.axis_index("row"), lax.axis_index("feat")
        def sources(chosen):
            table = [[source(r, *slot) for slot in chosen] for r in range(rows_n)]
            return jnp.asarray(table, jnp.int32)[row]

        apart = feat ^ (row // per_feat)
        fixed = [row % per_feat, apart == 0, apart % 2 == 0, row, feat]
        scalars = jnp.concatenate([
            jnp.stack([jnp.asarray(x, jnp.int32) for x in fixed]),
            (jnp.asarray(relative, jnp.int32) ^ feat) * (row_block // feats_n),
            sources(slots),
            sources(white_slots),
        ])
        first_place = STARTS + feats_n
        first_white = first_place + rows_n

        def pieces_of(chosen):
            return [p for slot in chosen for p in chunks[slot]]

        def column_far(mine):
            for bit in reversed(far_bits):
                got = send(mine, perm(
                    lambda r, f: (r, f ^ bit),
                    lambda r, f: (f ^ (r // per_feat)) % (2 * bit) == 0,
                ))
                if len(far_bits) > 1:
                    mine = got = jnp.where(apart % (2 * bit) == 0, mine, got)
            return got

        def to_far(near):
            keep, away = halve(scalars, *near)
            for bit in far_bits[:-1]:
                keep, away = halve(scalars, keep, swap(away, 0, bit))
            return keep, swap(away, 0, far_bits[-1])

        chunks = {(0, 0): [candidates]}
        columns, far_columns, white, near, far = [], [], [], [], []
        for k in range(hi_n + 1):
            fresh, out = [], {}
            if k > 0:
                last = k == hi_n - 1
                picked = pick(scalars, pieces_of(groups[k - 1]), row_block, half if last else 0)
                columns.append(picked[0])
            if k < hi_n - 1:
                fresh.append((k + 1, 0))
                chunks[k + 1, 0] = [send(chunks[k, 0][0], hi_pairs)]
                held = chunks[k, 0][0]
                for s in range(1, lo_n):
                    fresh.append((k, s))
                    held = send(held, lo_pairs)
                    chunks[k, s] = [held]
            elif k < hi_n:
                held = picked[1]
                for s in range(1, lo_n):
                    fresh.append((k, s))
                    held = send(held, lo_pairs)
                    chunks[k, s] = [held, send(picked[1 + s], hi_pairs)]
            out["fresh"] = [chunks[slot] for slot in fresh]
            if k == 0:
                out["scalars"] = touch(scalars, inv_factor)
            if k > 0:
                out["column"] = column_far(columns[-1])
                out["white"] = whiten(scalars, feats_n, inv_factor, pieces_of(white_groups[k - 1]))
            if k > 1:
                keep, away = white[k - 2]
                out["near"] = keep, swap(away, 0, 1)
            if k > 2:
                out["far"] = to_far(near[k - 3])
            out = fence(out)
            for slot, value in zip(fresh, out["fresh"]):
                chunks[slot] = value
            scalars = out.get("scalars", scalars)
            for name, kept in (("column", far_columns), ("white", white), ("near", near), ("far", far)):
                if name in out:
                    kept.append(out[name])
        keep, away = white[-1]
        packed = pack(scalars, columns, far_columns)
        last, before, packed = fence(((keep, swap(away, 0, 1)), to_far(near[-1]), packed))
        far.append(before)
        last, beside = fence((to_far(last), swap(packed, 0, 1)))
        far.append(last)
        sizes = [len(g) for g in white_groups]
        total = squares(scalars, first_white, weights[None], strata[None], far, sizes)
        total = fence(total + swap(total, 0, 1))
        column_t = join(scalars, packed, beside)
        bits = [(0, bit) for bit in far_bits] + [(bit, 0) for bit in row_bits]
        for i, bit in enumerate(bits):
            total = total + swap(total, *bit)
            if i == 0:
                total, column_t = fence((total, column_t))

        origins = []
        for i, slot in enumerate(slots):
            first = 0
            for piece in chunks[slot]:
                origins.append((first_place + i, first))
                first += piece.shape[0]
        information, new_weight, leverage = increment(
            scalars, origins, total, column_t, pieces_of(slots), features
        )
        return (new_weight.reshape(rows_dev), leverage.reshape(rows_dev), information)

    return per_device


def solution(mesh):
    in_specs = (P("row", "feat"), P("row", "feat"), P("row"), P("row"))
    out_specs = (P("row"), P("row"), P("row", "feat"))
    return jax.shard_map(
        make(mesh), mesh=mesh, in_specs=in_specs, out_specs=out_specs, check_vma=False
    )
```

```python
import functools

import jax
import jax.numpy as jnp
from jax import lax
from jax.experimental import pallas as pl
from jax.experimental.pallas import tpu as pltpu
from jax.sharding import PartitionSpec as P

BOTH = ("row", "feat")
HI = 4
MIB = 1 << 20
LANES = 128
BIG = 56
BLOCK, NEAR, EVEN, ROW, FEAT, STARTS = range(6)


def ring_order(count):
    return list(range(0, count, 2)) + list(range(1, count, 2))[::-1]


def ring_next(count):
    order = ring_order(count)
    return {order[i]: order[(i + 1) % count] for i in range(count)}


def call(kernel, name, out_shape, scratch, args, fixed=(), vmem=16, flops=1000):
    on_vmem = pl.BlockSpec(memory_space=pltpu.VMEM)
    on_hbm = pl.BlockSpec(memory_space=pltpu.HBM)
    scalars, rest = args
    out_hbm = "out" in fixed
    held = [x for x in fixed if not isinstance(x, str)]
    return pl.pallas_call(
        kernel,
        in_specs=[pl.BlockSpec(memory_space=pltpu.SMEM)] + [on_hbm] * len(held) + [on_vmem] * len(rest),
        out_specs=jax.tree.map(lambda _: on_hbm if out_hbm else on_vmem, out_shape),
        out_shape=out_shape,
        scratch_shapes=scratch,
        compiler_params=pltpu.CompilerParams(vmem_limit_bytes=vmem * MIB),
        cost_estimate=pl.CostEstimate(flops=flops, bytes_accessed=1000, transcendentals=0),
        name=name,
    )(scalars, *held, *rest)


def touch_kernel(scalars_ref, f_ref, out_ref):
    for i in range(scalars_ref.shape[0]):
        out_ref[i] = scalars_ref[i]


def touch(scalars, inv_factor):
    return pl.pallas_call(
        touch_kernel,
        in_specs=[pl.BlockSpec(memory_space=pltpu.SMEM), pl.BlockSpec(memory_space=pltpu.VMEM)],
        out_specs=pl.BlockSpec(memory_space=pltpu.SMEM),
        out_shape=jax.ShapeDtypeStruct(scalars.shape, scalars.dtype),
        compiler_params=pltpu.CompilerParams(vmem_limit_bytes=16 * MIB),
        cost_estimate=pl.CostEstimate(flops=1000, bytes_accessed=1000, transcendentals=0),
        name="touch",
    )(scalars, inv_factor)


def whiten_kernel(blocks, before, scalars_ref, f_ref, *refs):
    earlier, pieces, (keep_ref, away_ref, x_ref, xt_ref) = refs[:before], refs[before:-4], refs[-4:]
    place = 0
    for piece in pieces:
        x_ref[pl.ds(place, piece.shape[0]), :] = piece[...]
        place += piece.shape[0]
    wide = min(512, x_ref.shape[1])
    for c in range(x_ref.shape[1] // wide):
        xt_ref[pl.ds(c * wide, wide), :] = x_ref[:, c * wide:(c + 1) * wide].T
    tile = f_ref.shape[0] // blocks
    done = 0
    if before:
        done = earlier[0].shape[1]
        keep_ref[:, :done] = earlier[0][...]
        away_ref[:, :done] = earlier[1][...]

    def product(t):
        start = pl.multiple_of(scalars_ref[STARTS + t], tile)
        return jnp.dot(f_ref[pl.ds(start, tile), :], xt_ref[...], preferred_element_type=jnp.float32)

    def step(t, carry):
        place = pl.multiple_of(t * tile, tile)
        away_ref[pl.ds(place, tile), done:] = product(blocks // 2 + t).astype(jnp.bfloat16)
        keep_ref[pl.ds(place, tile), done:] = product(t)
        return carry

    lax.fori_loop(0, blocks // 2, step, 0)


def whiten(scalars, blocks, inv_factor, pieces, earlier=()):
    row_block, feat_block = inv_factor.shape
    rows = sum(p.shape[0] for p in pieces)
    out = (row_block // 2, rows + (earlier[0].shape[1] if earlier else 0))
    return call(
        functools.partial(whiten_kernel, blocks, len(earlier)),
        "whiten",
        [jax.ShapeDtypeStruct(out, jnp.float32), jax.ShapeDtypeStruct(out, jnp.bfloat16)],
        [pltpu.VMEM((rows, feat_block), jnp.bfloat16), pltpu.VMEM((feat_block, rows), jnp.bfloat16)],
        (scalars, [inv_factor] + list(earlier) + pieces),
        flops=8 * row_block * feat_block * rows,
    )


def halve_kernel(_, part_ref, got_ref, keep_ref, away_ref):
    left = keep_ref.shape[0]
    keep_ref[...] = part_ref[:left, :] + got_ref[:left, :].astype(jnp.float32)
    away_ref[...] = (part_ref[left:, :] + got_ref[left:, :].astype(jnp.float32)).astype(jnp.bfloat16)


def halve(scalars, part, got):
    out = (part.shape[0] // 2, part.shape[1])
    return call(
        halve_kernel,
        "halve",
        [jax.ShapeDtypeStruct(out, jnp.float32), jax.ShapeDtypeStruct(out, jnp.bfloat16)],
        [],
        (scalars, [part, got]),
    )


def pick_kernel(count, half, scalars_ref, *refs):
    pieces, outs = refs[:count], refs[count:]
    width = outs[0].shape[1]
    start = pl.multiple_of(scalars_ref[BLOCK] * width, width)
    place = 0
    for piece in pieces:
        outs[0][pl.ds(place, piece.shape[0]), :] = piece[:, pl.ds(start, width)]
        place += piece.shape[0]
    if half:
        outs[1][...] = pieces[-1][:half, :]
        for out, piece in zip(outs[2:], pieces):
            out[...] = piece[half:, :]


def pick(scalars, pieces, width, half=0):
    rows = sum(p.shape[0] for p in pieces)
    out = [jax.ShapeDtypeStruct((rows, width), jnp.bfloat16)]
    if half:
        out += [jax.ShapeDtypeStruct((half, pieces[0].shape[1]), jnp.bfloat16)] * len(pieces)
    return call(
        functools.partial(pick_kernel, len(pieces), half), "pick", out, [], (scalars, pieces)
    )


def fetch(pairs, sems):
    copies = [pltpu.make_async_copy(a, b, sems.at[i]) for i, (a, b) in enumerate(pairs)]
    for copy in copies:
        copy.start()
    return copies


def pack_kernel(count, scalars_ref, *refs):
    out_ref, sems = refs[-2:]

    def copy(sources):
        place, pairs = 0, []
        for source in sources:
            pairs.append((source, out_ref.at[pl.ds(place, source.shape[0])]))
            place += source.shape[0]
        for one in fetch(pairs, sems):
            one.wait()

    @pl.when(scalars_ref[NEAR] == 1)
    def _():
        copy(refs[:count])

    @pl.when(scalars_ref[NEAR] == 0)
    def _():
        copy(refs[count:-2])


def pack(scalars, own, got):
    out = (sum(x.shape[0] for x in own), own[0].shape[1])
    return call(
        functools.partial(pack_kernel, len(own)),
        "pack",
        jax.ShapeDtypeStruct(out, jnp.bfloat16),
        [pltpu.SemaphoreType.DMA((len(own),))],
        (scalars, []),
        tuple(own + got),
        BIG,
    )


def join_kernel(first, scalars_ref, own_ref, other_ref, out_ref, x_ref, xt_ref, sems):
    columns = pl.ds(first, x_ref.shape[1])

    @pl.when(scalars_ref[EVEN] == 1)
    def _():
        fetch([(own_ref.at[:, columns], x_ref)], sems)[0].wait()

    @pl.when(scalars_ref[EVEN] == 0)
    def _():
        fetch([(other_ref.at[:, columns], x_ref)], sems)[0].wait()

    wide = min(256, x_ref.shape[1])
    for c in range(x_ref.shape[1] // wide):
        xt_ref[pl.ds(c * wide, wide), :] = x_ref[:, c * wide:(c + 1) * wide].T
    fetch([(xt_ref, out_ref)], sems)[0].wait()


def join(scalars, own, other, half):
    rows, width = own.shape[0], own.shape[1] // 2
    return call(
        functools.partial(join_kernel, half * width),
        "join",
        jax.ShapeDtypeStruct((width, rows), jnp.bfloat16),
        [
            pltpu.VMEM((rows, width), jnp.bfloat16),
            pltpu.VMEM((width, rows), jnp.bfloat16),
            pltpu.SemaphoreType.DMA((1,)),
        ],
        (scalars, []),
        (own, other, "out"),
        BIG,
    )


def put_squares(out_ref, scalars_ref, slot, part_ref, other_ref):
    count = out_ref.shape[1]
    value = part_ref[...] + other_ref[...].astype(jnp.float32)
    line = jnp.sum(value * value, axis=0, keepdims=True)
    for i in range(line.shape[1] // count):
        out_ref[pl.ds(scalars_ref[slot + i], 1), :] = line[:, i * count:(i + 1) * count]


def early_kernel(slots, firsts, scalars_ref, *refs):
    early = 2 * len(firsts) - 2
    held = refs[early + 5:-1]
    w_ref, strata_ref, keep_ref, got_ref, out_ref = refs[early:early + 5]
    copies = fetch(list(zip(refs[:early], held)), refs[-1])
    out_ref[...] = jnp.zeros_like(out_ref)

    @pl.when(scalars_ref[FEAT] == 0)
    def _():
        out_ref[pl.ds(slots + scalars_ref[ROW], 1), :] = w_ref[...]
        out_ref[pl.ds(2 * slots + scalars_ref[ROW], 1), :] = strata_ref[...].astype(jnp.float32)

    put_squares(out_ref, scalars_ref, firsts[-1], keep_ref, got_ref)
    for copy in copies:
        copy.wait()
    for g, first in enumerate(firsts[:-1]):
        put_squares(out_ref, scalars_ref, first, held[2 * g], held[2 * g + 1])


def early_squares(scalars, firsts, slots, weights, strata, pairs):
    early = [x for pair in pairs[:-1] for x in pair]
    return call(
        functools.partial(early_kernel, slots, firsts),
        "early_squares",
        jax.ShapeDtypeStruct((3 * slots, weights.shape[1]), jnp.float32),
        [pltpu.VMEM(x.shape, x.dtype) for x in early] + [pltpu.SemaphoreType.DMA((len(early),))],
        (scalars, [weights, strata] + list(pairs[-1])),
        tuple(early),
        BIG,
    )


def last_kernel(first, scalars_ref, sums_ref, keep_ref, got_ref, out_ref):
    out_ref[...] = sums_ref[...]
    put_squares(out_ref, scalars_ref, first, keep_ref, got_ref)


def last_squares(scalars, first, sums, pair):
    return call(
        functools.partial(last_kernel, first),
        "last_squares",
        jax.ShapeDtypeStruct(sums.shape, jnp.float32),
        [],
        (scalars, [sums] + list(pair)),
    )


def weight_step(strata_n, features, row, sums_ref, new_ref, lev_ref, all_ref, d_ref):
    groups = sums_ref.shape[0] // 3
    raw, weights, strata = [sums_ref[pl.ds(i * groups, groups), :] for i in range(3)]
    products = weights * raw
    ratio = jnp.zeros_like(raw)
    for s in range(strata_n):
        inside = strata == float(s)
        mass = jnp.sum(jnp.where(inside, weights, 0.0), keepdims=True)
        product = jnp.sum(jnp.where(inside, products, 0.0), keepdims=True)
        ratio = jnp.where(inside, mass / product, ratio)
    new = products * ratio
    all_ref[...] = new
    new_ref[...] = all_ref[pl.ds(row, 1), :]
    lev_ref[...] = sums_ref[pl.ds(row, 1), :] / features
    step = new - weights
    count = step.shape[1]
    for g in range(groups):
        d_ref[pl.ds(g * count, count), :] = jnp.broadcast_to(step[g:g + 1, :], (LANES, count)).T


def information_kernel(features, pieces_of, scalars_ref, low_hbm, high_hbm, *refs):
    n = len(pieces_of)
    pieces, (sums_ref, got_ref, out_ref, new_ref, lev_ref) = refs[:n], refs[n:n + 5]
    all_ref, total_ref, d_ref, col_ref, p_ref, s_ref, buf_ref, col_sems, first_sems, rest_sems, sems = refs[n + 5:]
    width = s_ref.shape[1]
    steps = out_ref.shape[1] // width
    count = sums_ref.shape[1]
    sizes = [piece.shape[0] for piece in pieces]
    offsets = [sum(sizes[:i]) for i in range(n)]

    def bring(start, size):
        columns = pl.ds(start, size)
        return [
            (piece.at[:, columns], p_ref.at[pl.ds(offset, rows), columns])
            for piece, offset, rows in zip(pieces, offsets, sizes)
        ]

    def copy(j):
        slot = lax.rem(j, 2)
        return pltpu.make_async_copy(
            buf_ref.at[slot], out_ref.at[:, pl.ds(pl.multiple_of(j * width, width), width)], sems.at[slot]
        )

    half = col_ref.shape[0] // 2
    first = fetch(bring(0, width), first_sems)
    first += fetch([(low_hbm, col_ref.at[:half]), (high_hbm, col_ref.at[half:])], col_sems)
    rest = fetch(bring(width, (steps - 1) * width), rest_sems) if steps > 1 else []
    total_ref[...] = sums_ref[...] + got_ref[...]
    weight_step(
        2 * (sums_ref.shape[0] // 3), features, scalars_ref[ROW], total_ref, new_ref, lev_ref, all_ref, d_ref
    )
    for one in first:
        one.wait()

    def step(j, carry):
        @pl.when(j == 1)
        def _():
            for one in rest:
                one.wait()

        for i, (slot, first) in enumerate(pieces_of):
            size = sizes[i]
            start = pl.multiple_of(scalars_ref[slot] * count + first, size)
            scale = d_ref[pl.ds(start, size), :]
            for c in range(width // LANES):
                start = pl.multiple_of(j * width + c * LANES, LANES)
                value = p_ref[pl.ds(offsets[i], size), pl.ds(start, LANES)].astype(jnp.float32)
                s_ref[pl.ds(offsets[i], size), c * LANES:(c + 1) * LANES] = (scale * value).astype(jnp.bfloat16)

        @pl.when(j > 1)
        def _():
            copy(j - 2).wait()

        buf_ref[lax.rem(j, 2)] = jnp.dot(col_ref[...], s_ref[...], preferred_element_type=jnp.float32)
        copy(j).start()
        return carry

    lax.fori_loop(0, steps, step, 0)
    for j in range(max(0, steps - 2), steps):
        copy(jnp.int32(j)).wait()


def increment(scalars, pieces_of, sums, got, columns_t, pieces, features):
    row_block, rows = 2 * columns_t[0].shape[0], columns_t[0].shape[1]
    groups, count = sums.shape[0] // 3, sums.shape[1]
    feat_block = pieces[0].shape[1]
    width = min(512, feat_block)
    steps = feat_block // width
    on_vmem = pl.BlockSpec(memory_space=pltpu.VMEM)
    on_hbm = pl.BlockSpec(memory_space=pltpu.HBM)
    return pl.pallas_call(
        functools.partial(information_kernel, features, pieces_of),
        in_specs=[pl.BlockSpec(memory_space=pltpu.SMEM)] + [on_hbm] * (2 + len(pieces)) + [on_vmem] * 2,
        out_specs=[on_hbm, on_vmem, on_vmem],
        out_shape=[
            jax.ShapeDtypeStruct((row_block, feat_block), jnp.float32),
            jax.ShapeDtypeStruct((1, count), jnp.float32),
            jax.ShapeDtypeStruct((1, count), jnp.float32),
        ],
        scratch_shapes=[
            pltpu.VMEM((groups, count), jnp.float32),
            pltpu.VMEM((3 * groups, count), jnp.float32),
            pltpu.VMEM((rows, LANES), jnp.float32),
            pltpu.VMEM((row_block, rows), jnp.bfloat16),
            pltpu.VMEM((rows, feat_block), jnp.bfloat16),
            pltpu.VMEM((rows, width), jnp.bfloat16),
            pltpu.VMEM((2, row_block, width), jnp.float32),
            pltpu.SemaphoreType.DMA((2,)),
            pltpu.SemaphoreType.DMA((len(pieces),)),
            pltpu.SemaphoreType.DMA((len(pieces),)),
            pltpu.SemaphoreType.DMA((2,)),
        ],
        compiler_params=pltpu.CompilerParams(vmem_limit_bytes=BIG * MIB),
        cost_estimate=pl.CostEstimate(
            flops=2 * row_block * feat_block * rows, bytes_accessed=1000, transcendentals=0
        ),
        name="increment",
    )(scalars, *columns_t, *pieces, sums, got)


def make(mesh):
    rows_n, feats_n = mesh.shape["row"], mesh.shape["feat"]
    hi_n = HI
    lo_n = rows_n // hi_n
    per_feat = rows_n // feats_n
    everyone = [(r, f) for r in range(rows_n) for f in range(feats_n)]

    def perm(target, keep=lambda r, f: True):
        out = []
        for r, f in everyone:
            if keep(r, f):
                r2, f2 = target(r, f)
                out.append((r * feats_n + f, r2 * feats_n + f2))
        return out

    def send(x, pairs):
        return lax.ppermute(x, BOTH, pairs)

    def swap(x, r_bit, f_bit):
        return send(x, perm(lambda r, f: (r ^ r_bit, f ^ f_bit)))

    fence = lax.optimization_barrier
    hi_next, lo_next = ring_next(hi_n), ring_next(lo_n)
    hi_pairs = perm(lambda r, f: (hi_next[r // lo_n] * lo_n + r % lo_n, f))
    lo_pairs = perm(lambda r, f: (r // lo_n * lo_n + lo_next[r % lo_n], f))
    hi_order, lo_order = ring_order(hi_n), ring_order(lo_n)

    def source(r, k, s):
        h, l = r // lo_n, r % lo_n
        h2 = hi_order[(hi_order.index(h) - k) % hi_n]
        l2 = lo_order[(lo_order.index(l) - s) % lo_n]
        return h2 * lo_n + l2

    feat_bits = [1 << b for b in range(feats_n.bit_length() - 1)]
    far_bits = feat_bits[1:]
    row_bits = [1 << b for b in range(rows_n.bit_length() - 1)]
    relative = [0]
    for bit in reversed(feat_bits):
        relative = relative + [j + bit for j in relative]

    groups = [[(0, s) for s in range(lo_n)] + [(1, 0)]]
    for k in range(1, hi_n):
        groups.append([(k, s) for s in range(1, lo_n)] + ([(k + 1, 0)] if k + 1 < hi_n else []))
    slots = [slot for group in groups for slot in group]
    white_groups = [[(k, s) for k in ks for s in range(lo_n)] for ks in [[0, 1]] + [[k] for k in range(2, hi_n)]]
    white_slots = [slot for group in white_groups for slot in group]

    def per_device(candidates, inv_factor, weights, strata):
        rows_dev, feat_block = candidates.shape
        row_block = inv_factor.shape[0]
        features = feat_block * feats_n
        half = rows_dev // 2
        row, feat = lax.axis_index("row"), lax.axis_index("feat")
        def sources(chosen):
            table = [[source(r, *slot) for slot in chosen] for r in range(rows_n)]
            return jnp.asarray(table, jnp.int32)[row]

        apart = feat ^ (row // per_feat)
        fixed = [row % per_feat, apart == 0, apart % 2 == 0, row, feat]
        scalars = jnp.concatenate([
            jnp.stack([jnp.asarray(x, jnp.int32) for x in fixed]),
            (jnp.asarray(relative, jnp.int32) ^ feat) * (row_block // feats_n),
            sources(slots),
            sources(white_slots),
        ])
        first_place = STARTS + feats_n
        first_white = first_place + rows_n

        def pieces_of(chosen):
            return [p for slot in chosen for p in chunks[slot]]

        def column_far(mine):
            for bit in reversed(far_bits):
                got = send(mine, perm(
                    lambda r, f: (r, f ^ bit),
                    lambda r, f: (f ^ (r // per_feat)) % (2 * bit) == 0,
                ))
                if len(far_bits) > 1:
                    mine = got = jnp.where(apart % (2 * bit) == 0, mine, got)
            return got

        def to_far(near):
            keep, away = halve(scalars, *near)
            for bit in far_bits[:-1]:
                keep, away = halve(scalars, keep, swap(away, 0, bit))
            return keep, swap(away, 0, far_bits[-1])

        chunks = {(0, 0): [candidates]}
        columns, far_columns, white, near, far = [], [], [], [], []
        for k in range(hi_n + 1):
            fresh, out = [], {}
            if k > 0:
                last = k == hi_n - 1
                picked = pick(scalars, pieces_of(groups[k - 1]), row_block, half if last else 0)
                columns.append(picked[0])
            if k < hi_n - 1:
                fresh.append((k + 1, 0))
                chunks[k + 1, 0] = [send(chunks[k, 0][0], hi_pairs)]
                held = chunks[k, 0][0]
                for s in range(1, lo_n):
                    fresh.append((k, s))
                    held = send(held, lo_pairs)
                    chunks[k, s] = [held]
            elif k < hi_n:
                held = picked[1]
                for s in range(1, lo_n):
                    fresh.append((k, s))
                    held = send(held, lo_pairs)
                    chunks[k, s] = [held, send(picked[1 + s], hi_pairs)]
            out["fresh"] = [chunks[slot] for slot in fresh]
            if k == 0:
                out["scalars"] = touch(scalars, inv_factor)
            if k > 0:
                out["column"] = column_far(columns[-1])
                white_pieces = pieces_of([(k - 1, s) for s in range(lo_n)])
                earlier = white.pop() if k == 2 else ()
                out["white"] = whiten(scalars, feats_n, inv_factor, white_pieces, earlier)
            if k > 2:
                keep, away = white[k - 3]
                out["near"] = keep, swap(away, 0, 1)
            if k > 3:
                out["far"] = to_far(near[k - 4])
            out = fence(out)
            for slot, value in zip(fresh, out["fresh"]):
                chunks[slot] = value
            scalars = out.get("scalars", scalars)
            for name, kept in (("column", far_columns), ("white", white), ("near", near), ("far", far)):
                if name in out:
                    kept.append(out[name])
        keep, away = white[-1]
        packed = pack(scalars, columns, far_columns)
        last, before, packed = fence(((keep, swap(away, 0, 1)), to_far(near[-1]), packed))
        far.append(before)
        slots_n = len(white_slots)
        firsts = [first_white + sum(len(x) for x in white_groups[:g]) for g in range(len(white_groups))]
        sums = early_squares(scalars, firsts[:-1], slots_n, weights[None], strata[None], far)
        last, beside, sums = fence((to_far(last), swap(packed, 0, 1), sums))
        total = last_squares(scalars, firsts[-1], sums, last)
        total = fence(total + swap(total, 0, 1))
        columns_t = []
        bits = [(0, bit) for bit in far_bits] + [(bit, 0) for bit in row_bits]
        for bit in bits[:-1]:
            total = total + swap(total, *bit)
            if len(columns_t) < 2:
                columns_t.append(join(scalars, packed, beside, len(columns_t)))
                total, columns_t = fence((total, columns_t))
        got = swap(total, *bits[-1])
        origins = []
        for i, slot in enumerate(slots):
            first = 0
            for piece in chunks[slot]:
                origins.append((first_place + i, first))
                first += piece.shape[0]
        information, new_weight, leverage = increment(
            scalars, origins, total, got, columns_t, pieces_of(slots), features
        )
        return (new_weight.reshape(rows_dev), leverage.reshape(rows_dev), information)

    return per_device


def solution(mesh):
    in_specs = (P("row", "feat"), P("row", "feat"), P("row"), P("row"))
    out_specs = (P("row"), P("row"), P("row", "feat"))
    return jax.shard_map(
        make(mesh), mesh=mesh, in_specs=in_specs, out_specs=out_specs, check_vma=False
    )
```

```python
import functools

import jax
import jax.numpy as jnp
from jax import lax
from jax.experimental import pallas as pl
from jax.experimental.pallas import tpu as pltpu
from jax.sharding import PartitionSpec as P

BOTH = ("row", "feat")
HI = 4
MIB = 1 << 20
LANES = 128
BIG = 56
BLOCK, NEAR, EVEN, ROW, FEAT, STARTS = range(6)


def ring_order(count):
    return list(range(0, count, 2)) + list(range(1, count, 2))[::-1]


def ring_next(count):
    order = ring_order(count)
    return {order[i]: order[(i + 1) % count] for i in range(count)}


def call(kernel, name, out_shape, scratch, args, fixed=(), vmem=16, flops=1000):
    on_vmem = pl.BlockSpec(memory_space=pltpu.VMEM)
    on_hbm = pl.BlockSpec(memory_space=pltpu.HBM)
    scalars, rest = args
    out_hbm = "out" in fixed
    held = [x for x in fixed if not isinstance(x, str)]
    return pl.pallas_call(
        kernel,
        in_specs=[pl.BlockSpec(memory_space=pltpu.SMEM)] + [on_hbm] * len(held) + [on_vmem] * len(rest),
        out_specs=jax.tree.map(lambda _: on_hbm if out_hbm else on_vmem, out_shape),
        out_shape=out_shape,
        scratch_shapes=scratch,
        compiler_params=pltpu.CompilerParams(vmem_limit_bytes=vmem * MIB),
        cost_estimate=pl.CostEstimate(flops=flops, bytes_accessed=1000, transcendentals=0),
        name=name,
    )(scalars, *held, *rest)


def touch_kernel(scalars_ref, f_ref, out_ref):
    for i in range(scalars_ref.shape[0]):
        out_ref[i] = scalars_ref[i]


def touch(scalars, inv_factor):
    return pl.pallas_call(
        touch_kernel,
        in_specs=[pl.BlockSpec(memory_space=pltpu.SMEM), pl.BlockSpec(memory_space=pltpu.VMEM)],
        out_specs=pl.BlockSpec(memory_space=pltpu.SMEM),
        out_shape=jax.ShapeDtypeStruct(scalars.shape, scalars.dtype),
        compiler_params=pltpu.CompilerParams(vmem_limit_bytes=16 * MIB),
        cost_estimate=pl.CostEstimate(flops=1000, bytes_accessed=1000, transcendentals=0),
        name="touch",
    )(scalars, inv_factor)


def whiten_kernel(blocks, before, scalars_ref, f_ref, *refs):
    earlier, pieces, (keep_ref, away_ref, x_ref, xt_ref) = refs[:before], refs[before:-4], refs[-4:]
    place = 0
    for piece in pieces:
        x_ref[pl.ds(place, piece.shape[0]), :] = piece[...]
        place += piece.shape[0]
    wide = min(512, x_ref.shape[1])
    for c in range(x_ref.shape[1] // wide):
        xt_ref[pl.ds(c * wide, wide), :] = x_ref[:, c * wide:(c + 1) * wide].T
    tile = f_ref.shape[0] // blocks
    done = 0
    if before:
        done = earlier[0].shape[1]
        keep_ref[:, :done] = earlier[0][...]
        away_ref[:, :done] = earlier[1][...]

    def product(t):
        start = pl.multiple_of(scalars_ref[STARTS + t], tile)
        return jnp.dot(f_ref[pl.ds(start, tile), :], xt_ref[...], preferred_element_type=jnp.float32)

    def step(t, carry):
        place = pl.multiple_of(t * tile, tile)
        away_ref[pl.ds(place, tile), done:] = product(blocks // 2 + t).astype(jnp.bfloat16)
        keep_ref[pl.ds(place, tile), done:] = product(t)
        return carry

    lax.fori_loop(0, blocks // 2, step, 0)


def whiten(scalars, blocks, inv_factor, pieces, earlier=()):
    row_block, feat_block = inv_factor.shape
    rows = sum(p.shape[0] for p in pieces)
    out = (row_block // 2, rows + (earlier[0].shape[1] if earlier else 0))
    return call(
        functools.partial(whiten_kernel, blocks, len(earlier)),
        "whiten",
        [jax.ShapeDtypeStruct(out, jnp.float32), jax.ShapeDtypeStruct(out, jnp.bfloat16)],
        [pltpu.VMEM((rows, feat_block), jnp.bfloat16), pltpu.VMEM((feat_block, rows), jnp.bfloat16)],
        (scalars, [inv_factor] + list(earlier) + pieces),
        flops=8 * row_block * feat_block * rows,
    )


def halve_kernel(_, part_ref, got_ref, keep_ref, away_ref):
    left = keep_ref.shape[0]
    keep_ref[...] = part_ref[:left, :] + got_ref[:left, :].astype(jnp.float32)
    away_ref[...] = (part_ref[left:, :] + got_ref[left:, :].astype(jnp.float32)).astype(jnp.bfloat16)


def halve(scalars, part, got):
    out = (part.shape[0] // 2, part.shape[1])
    return call(
        halve_kernel,
        "halve",
        [jax.ShapeDtypeStruct(out, jnp.float32), jax.ShapeDtypeStruct(out, jnp.bfloat16)],
        [],
        (scalars, [part, got]),
    )


def pick_kernel(count, half, scalars_ref, *refs):
    pieces, outs = refs[:count], refs[count:]
    width = outs[0].shape[1]
    start = pl.multiple_of(scalars_ref[BLOCK] * width, width)
    place = 0
    for piece in pieces:
        outs[0][pl.ds(place, piece.shape[0]), :] = piece[:, pl.ds(start, width)]
        place += piece.shape[0]
    if half:
        outs[1][...] = pieces[-1][:half, :]
        for out, piece in zip(outs[2:], pieces):
            out[...] = piece[half:, :]


def pick(scalars, pieces, width, half=0):
    rows = sum(p.shape[0] for p in pieces)
    out = [jax.ShapeDtypeStruct((rows, width), jnp.bfloat16)]
    if half:
        out += [jax.ShapeDtypeStruct((half, pieces[0].shape[1]), jnp.bfloat16)] * len(pieces)
    return call(
        functools.partial(pick_kernel, len(pieces), half), "pick", out, [], (scalars, pieces)
    )


def fetch(pairs, sems):
    copies = [pltpu.make_async_copy(a, b, sems.at[i]) for i, (a, b) in enumerate(pairs)]
    for copy in copies:
        copy.start()
    return copies


def pack_kernel(count, scalars_ref, *refs):
    out_ref, sems = refs[-2:]

    def copy(sources):
        place, pairs = 0, []
        for source in sources:
            pairs.append((source, out_ref.at[pl.ds(place, source.shape[0])]))
            place += source.shape[0]
        for one in fetch(pairs, sems):
            one.wait()

    @pl.when(scalars_ref[NEAR] == 1)
    def _():
        copy(refs[:count])

    @pl.when(scalars_ref[NEAR] == 0)
    def _():
        copy(refs[count:-2])


def pack(scalars, own, got):
    out = (sum(x.shape[0] for x in own), own[0].shape[1])
    return call(
        functools.partial(pack_kernel, len(own)),
        "pack",
        jax.ShapeDtypeStruct(out, jnp.bfloat16),
        [pltpu.SemaphoreType.DMA((len(own),))],
        (scalars, []),
        tuple(own + got),
        BIG,
    )


def join_kernel(first, scalars_ref, own_ref, other_ref, out_ref, x_ref, xt_ref, in_sems, out_sems):
    wide = min(256, x_ref.shape[1])
    parts = [pl.ds(c * wide, wide) for c in range(x_ref.shape[1] // wide)]

    def turn(source):
        arriving = fetch(
            [(source.at[:, pl.ds(first + c * wide, wide)], x_ref.at[:, part]) for c, part in enumerate(parts)],
            in_sems,
        )
        leaving = []
        for c, part in enumerate(parts):
            arriving[c].wait()
            xt_ref[part, :] = x_ref[:, part].T
            leaving += fetch([(xt_ref.at[part], out_ref.at[part])], out_sems.at[pl.ds(c, 1)])
        for one in leaving:
            one.wait()

    @pl.when(scalars_ref[EVEN] == 1)
    def _():
        turn(own_ref)

    @pl.when(scalars_ref[EVEN] == 0)
    def _():
        turn(other_ref)


def join(scalars, own, other, half):
    rows, width = own.shape[0], own.shape[1] // 2
    return call(
        functools.partial(join_kernel, half * width),
        "join",
        jax.ShapeDtypeStruct((width, rows), jnp.bfloat16),
        [
            pltpu.VMEM((rows, width), jnp.bfloat16),
            pltpu.VMEM((width, rows), jnp.bfloat16),
            pltpu.SemaphoreType.DMA((max(1, width // 256),)),
            pltpu.SemaphoreType.DMA((max(1, width // 256),)),
        ],
        (scalars, []),
        (own, other, "out"),
        BIG,
    )


def put_squares(out_ref, scalars_ref, slot, part_ref, other_ref):
    count = out_ref.shape[1]
    value = part_ref[...] + other_ref[...].astype(jnp.float32)
    line = jnp.sum(value * value, axis=0, keepdims=True)
    for i in range(line.shape[1] // count):
        out_ref[pl.ds(scalars_ref[slot + i], 1), :] = line[:, i * count:(i + 1) * count]


def early_kernel(slots, firsts, scalars_ref, w_ref, strata_ref, *refs):
    out_ref = refs[-1]
    out_ref[...] = jnp.zeros_like(out_ref)

    @pl.when(scalars_ref[FEAT] == 0)
    def _():
        out_ref[pl.ds(slots + scalars_ref[ROW], 1), :] = w_ref[...]
        out_ref[pl.ds(2 * slots + scalars_ref[ROW], 1), :] = strata_ref[...].astype(jnp.float32)

    for g, first in enumerate(firsts):
        put_squares(out_ref, scalars_ref, first, refs[2 * g], refs[2 * g + 1])


def early_squares(scalars, firsts, slots, weights, strata, pairs):
    return call(
        functools.partial(early_kernel, slots, firsts),
        "early_squares",
        jax.ShapeDtypeStruct((3 * slots, weights.shape[1]), jnp.float32),
        [],
        (scalars, [weights, strata] + [x for pair in pairs for x in pair]),
    )


def last_kernel(first, scalars_ref, sums_ref, keep_ref, got_ref, out_ref):
    out_ref[...] = sums_ref[...]
    put_squares(out_ref, scalars_ref, first, keep_ref, got_ref)


def last_squares(scalars, first, sums, pair):
    return call(
        functools.partial(last_kernel, first),
        "last_squares",
        jax.ShapeDtypeStruct(sums.shape, jnp.float32),
        [],
        (scalars, [sums] + list(pair)),
    )


def weight_step(strata_n, features, row, sums_ref, new_ref, lev_ref, all_ref, d_ref):
    groups = sums_ref.shape[0] // 3
    raw, weights, strata = [sums_ref[pl.ds(i * groups, groups), :] for i in range(3)]
    products = weights * raw
    ratio = jnp.zeros_like(raw)
    for s in range(strata_n):
        inside = strata == float(s)
        mass = jnp.sum(jnp.where(inside, weights, 0.0), keepdims=True)
        product = jnp.sum(jnp.where(inside, products, 0.0), keepdims=True)
        ratio = jnp.where(inside, mass / product, ratio)
    new = products * ratio
    all_ref[...] = new
    new_ref[...] = all_ref[pl.ds(row, 1), :]
    lev_ref[...] = sums_ref[pl.ds(row, 1), :] / features
    step = new - weights
    count = step.shape[1]
    for g in range(groups):
        d_ref[pl.ds(g * count, count), :] = jnp.broadcast_to(step[g:g + 1, :], (LANES, count)).T


def information_kernel(features, pieces_of, scalars_ref, low_hbm, high_hbm, *refs):
    n = len(pieces_of)
    pieces, (sums_ref, got_ref, out_ref, new_ref, lev_ref) = refs[:n], refs[n:n + 5]
    all_ref, total_ref, d_ref, col_ref, p_ref, s_ref, buf_ref, col_sems, first_sems, rest_sems, sems = refs[n + 5:]
    width = s_ref.shape[1]
    steps = out_ref.shape[1] // width
    count = sums_ref.shape[1]
    sizes = [piece.shape[0] for piece in pieces]
    offsets = [sum(sizes[:i]) for i in range(n)]

    def bring(start, size):
        columns = pl.ds(start, size)
        return [
            (piece.at[:, columns], p_ref.at[pl.ds(offset, rows), columns])
            for piece, offset, rows in zip(pieces, offsets, sizes)
        ]

    def copy(j):
        slot = lax.rem(j, 2)
        return pltpu.make_async_copy(
            buf_ref.at[slot], out_ref.at[:, pl.ds(pl.multiple_of(j * width, width), width)], sems.at[slot]
        )

    half = col_ref.shape[0] // 2
    first = fetch(bring(0, width), first_sems)
    first += fetch([(low_hbm, col_ref.at[:half]), (high_hbm, col_ref.at[half:])], col_sems)
    total_ref[...] = sums_ref[...] + got_ref[...]
    weight_step(
        2 * (sums_ref.shape[0] // 3), features, scalars_ref[ROW], total_ref, new_ref, lev_ref, all_ref, d_ref
    )
    for one in first:
        one.wait()
    rest = fetch(bring(width, (steps - 1) * width), rest_sems) if steps > 1 else []

    def step(j, carry):
        @pl.when(j == 1)
        def _():
            for one in rest:
                one.wait()

        for i, (slot, first) in enumerate(pieces_of):
            size = sizes[i]
            start = pl.multiple_of(scalars_ref[slot] * count + first, size)
            scale = d_ref[pl.ds(start, size), :]
            for c in range(width // LANES):
                start = pl.multiple_of(j * width + c * LANES, LANES)
                value = p_ref[pl.ds(offsets[i], size), pl.ds(start, LANES)].astype(jnp.float32)
                s_ref[pl.ds(offsets[i], size), c * LANES:(c + 1) * LANES] = (scale * value).astype(jnp.bfloat16)

        @pl.when(j > 1)
        def _():
            copy(j - 2).wait()

        buf_ref[lax.rem(j, 2)] = jnp.dot(col_ref[...], s_ref[...], preferred_element_type=jnp.float32)
        copy(j).start()
        return carry

    lax.fori_loop(0, steps, step, 0)
    for j in range(max(0, steps - 2), steps):
        copy(jnp.int32(j)).wait()


def increment(scalars, pieces_of, sums, got, columns_t, pieces, features):
    row_block, rows = 2 * columns_t[0].shape[0], columns_t[0].shape[1]
    groups, count = sums.shape[0] // 3, sums.shape[1]
    feat_block = pieces[0].shape[1]
    width = min(512, feat_block)
    steps = feat_block // width
    on_vmem = pl.BlockSpec(memory_space=pltpu.VMEM)
    on_hbm = pl.BlockSpec(memory_space=pltpu.HBM)
    return pl.pallas_call(
        functools.partial(information_kernel, features, pieces_of),
        in_specs=[pl.BlockSpec(memory_space=pltpu.SMEM)] + [on_hbm] * (2 + len(pieces)) + [on_vmem] * 2,
        out_specs=[on_hbm, on_vmem, on_vmem],
        out_shape=[
            jax.ShapeDtypeStruct((row_block, feat_block), jnp.float32),
            jax.ShapeDtypeStruct((1, count), jnp.float32),
            jax.ShapeDtypeStruct((1, count), jnp.float32),
        ],
        scratch_shapes=[
            pltpu.VMEM((groups, count), jnp.float32),
            pltpu.VMEM((3 * groups, count), jnp.float32),
            pltpu.VMEM((rows, LANES), jnp.float32),
            pltpu.VMEM((row_block, rows), jnp.bfloat16),
            pltpu.VMEM((rows, feat_block), jnp.bfloat16),
            pltpu.VMEM((rows, width), jnp.bfloat16),
            pltpu.VMEM((2, row_block, width), jnp.float32),
            pltpu.SemaphoreType.DMA((2,)),
            pltpu.SemaphoreType.DMA((len(pieces),)),
            pltpu.SemaphoreType.DMA((len(pieces),)),
            pltpu.SemaphoreType.DMA((2,)),
        ],
        compiler_params=pltpu.CompilerParams(vmem_limit_bytes=BIG * MIB),
        cost_estimate=pl.CostEstimate(
            flops=2 * row_block * feat_block * rows, bytes_accessed=1000, transcendentals=0
        ),
        name="increment",
    )(scalars, *columns_t, *pieces, sums, got)


def make(mesh):
    rows_n, feats_n = mesh.shape["row"], mesh.shape["feat"]
    hi_n = HI
    lo_n = rows_n // hi_n
    per_feat = rows_n // feats_n
    everyone = [(r, f) for r in range(rows_n) for f in range(feats_n)]

    def perm(target, keep=lambda r, f: True):
        out = []
        for r, f in everyone:
            if keep(r, f):
                r2, f2 = target(r, f)
                out.append((r * feats_n + f, r2 * feats_n + f2))
        return out

    def send(x, pairs):
        return lax.ppermute(x, BOTH, pairs)

    def swap(x, r_bit, f_bit):
        return send(x, perm(lambda r, f: (r ^ r_bit, f ^ f_bit)))

    fence = lax.optimization_barrier
    hi_next, lo_next = ring_next(hi_n), ring_next(lo_n)
    hi_pairs = perm(lambda r, f: (hi_next[r // lo_n] * lo_n + r % lo_n, f))
    lo_pairs = perm(lambda r, f: (r // lo_n * lo_n + lo_next[r % lo_n], f))
    hi_order, lo_order = ring_order(hi_n), ring_order(lo_n)

    def source(r, k, s):
        h, l = r // lo_n, r % lo_n
        h2 = hi_order[(hi_order.index(h) - k) % hi_n]
        l2 = lo_order[(lo_order.index(l) - s) % lo_n]
        return h2 * lo_n + l2

    feat_bits = [1 << b for b in range(feats_n.bit_length() - 1)]
    far_bits = feat_bits[1:]
    row_bits = [1 << b for b in range(rows_n.bit_length() - 1)]
    relative = [0]
    for bit in reversed(feat_bits):
        relative = relative + [j + bit for j in relative]

    groups = [[(0, s) for s in range(lo_n)] + [(1, 0)]]
    for k in range(1, hi_n):
        groups.append([(k, s) for s in range(1, lo_n)] + ([(k + 1, 0)] if k + 1 < hi_n else []))
    slots = [slot for group in groups for slot in group]
    white_groups = [[(k, s) for k in ks for s in range(lo_n)] for ks in [[0, 1]] + [[k] for k in range(2, hi_n)]]
    white_slots = [slot for group in white_groups for slot in group]

    def per_device(candidates, inv_factor, weights, strata):
        rows_dev, feat_block = candidates.shape
        row_block = inv_factor.shape[0]
        features = feat_block * feats_n
        half = rows_dev // 2
        row, feat = lax.axis_index("row"), lax.axis_index("feat")
        def sources(chosen):
            table = [[source(r, *slot) for slot in chosen] for r in range(rows_n)]
            return jnp.asarray(table, jnp.int32)[row]

        apart = feat ^ (row // per_feat)
        fixed = [row % per_feat, apart == 0, apart % 2 == 0, row, feat]
        scalars = jnp.concatenate([
            jnp.stack([jnp.asarray(x, jnp.int32) for x in fixed]),
            (jnp.asarray(relative, jnp.int32) ^ feat) * (row_block // feats_n),
            sources(slots),
            sources(white_slots),
        ])
        first_place = STARTS + feats_n
        first_white = first_place + rows_n

        def pieces_of(chosen):
            return [p for slot in chosen for p in chunks[slot]]

        def column_far(mine):
            for bit in reversed(far_bits):
                got = send(mine, perm(
                    lambda r, f: (r, f ^ bit),
                    lambda r, f: (f ^ (r // per_feat)) % (2 * bit) == 0,
                ))
                if len(far_bits) > 1:
                    mine = got = jnp.where(apart % (2 * bit) == 0, mine, got)
            return got

        def to_far(near):
            keep, away = halve(scalars, *near)
            for bit in far_bits[:-1]:
                keep, away = halve(scalars, keep, swap(away, 0, bit))
            return keep, swap(away, 0, far_bits[-1])

        chunks = {(0, 0): [candidates]}
        columns, far_columns, white, near, far = [], [], [], [], []
        for k in range(hi_n + 1):
            fresh, out = [], {}
            if k > 0:
                last = k == hi_n - 1
                picked = pick(scalars, pieces_of(groups[k - 1]), row_block, half if last else 0)
                columns.append(picked[0])
            if k < hi_n - 1:
                fresh.append((k + 1, 0))
                chunks[k + 1, 0] = [send(chunks[k, 0][0], hi_pairs)]
                held = chunks[k, 0][0]
                for s in range(1, lo_n):
                    fresh.append((k, s))
                    held = send(held, lo_pairs)
                    chunks[k, s] = [held]
            elif k < hi_n:
                held = picked[1]
                for s in range(1, lo_n):
                    fresh.append((k, s))
                    held = send(held, lo_pairs)
                    chunks[k, s] = [held, send(picked[1 + s], hi_pairs)]
            out["fresh"] = [chunks[slot] for slot in fresh]
            if k == 0:
                out["scalars"] = touch(scalars, inv_factor)
            if k > 0:
                out["column"] = column_far(columns[-1])
                white_pieces = pieces_of([(k - 1, s) for s in range(lo_n)])
                earlier = white.pop() if k == 2 else ()
                out["white"] = whiten(scalars, feats_n, inv_factor, white_pieces, earlier)
            if k > 2:
                keep, away = white[k - 3]
                out["near"] = keep, swap(away, 0, 1)
            if k > 3:
                out["far"] = to_far(near[k - 4])
            out = fence(out)
            for slot, value in zip(fresh, out["fresh"]):
                chunks[slot] = value
            scalars = out.get("scalars", scalars)
            for name, kept in (("column", far_columns), ("white", white), ("near", near), ("far", far)):
                if name in out:
                    kept.append(out[name])
        keep, away = white[-1]
        packed = pack(scalars, columns, far_columns)
        last, before, packed = fence(((keep, swap(away, 0, 1)), to_far(near[-1]), packed))
        far.append(before)
        slots_n = len(white_slots)
        firsts = [first_white + sum(len(x) for x in white_groups[:g]) for g in range(len(white_groups))]
        sums = early_squares(scalars, firsts[:-1], slots_n, weights[None], strata[None], far)
        last, beside, sums = fence((to_far(last), swap(packed, 0, 1), sums))
        total = last_squares(scalars, firsts[-1], sums, last)
        total = fence(total + swap(total, 0, 1))
        columns_t = []
        bits = [(0, bit) for bit in far_bits] + [(bit, 0) for bit in row_bits]
        for bit in bits[:-1]:
            total = total + swap(total, *bit)
            if len(columns_t) < 2:
                columns_t.append(join(scalars, packed, beside, len(columns_t)))
                total, columns_t = fence((total, columns_t))
        got = swap(total, *bits[-1])
        origins = []
        for i, slot in enumerate(slots):
            first = 0
            for piece in chunks[slot]:
                origins.append((first_place + i, first))
                first += piece.shape[0]
        information, new_weight, leverage = increment(
            scalars, origins, total, got, columns_t, pieces_of(slots), features
        )
        return (new_weight.reshape(rows_dev), leverage.reshape(rows_dev), information)

    return per_device


def solution(mesh):
    in_specs = (P("row", "feat"), P("row", "feat"), P("row"), P("row"))
    out_specs = (P("row"), P("row"), P("row", "feat"))
    return jax.shard_map(
        make(mesh), mesh=mesh, in_specs=in_specs, out_specs=out_specs, check_vma=False
    )
```

```python
import functools

import jax
import jax.numpy as jnp
from jax import lax
from jax.experimental import pallas as pl
from jax.experimental.pallas import tpu as pltpu
from jax.sharding import PartitionSpec as P

BOTH = ("row", "feat")
HI = 4
MIB = 1 << 20
LANES = 128
BIG = 56
BLOCK, NEAR, EVEN, ROW, FEAT, STARTS = range(6)


def ring_order(count):
    return list(range(0, count, 2)) + list(range(1, count, 2))[::-1]


def ring_next(count):
    order = ring_order(count)
    return {order[i]: order[(i + 1) % count] for i in range(count)}


def call(kernel, name, out_shape, scratch, args, fixed=(), vmem=16, flops=1000):
    on_vmem = pl.BlockSpec(memory_space=pltpu.VMEM)
    on_hbm = pl.BlockSpec(memory_space=pltpu.HBM)
    scalars, rest = args
    out_hbm = "out" in fixed
    held = [x for x in fixed if not isinstance(x, str)]
    return pl.pallas_call(
        kernel,
        in_specs=[pl.BlockSpec(memory_space=pltpu.SMEM)] + [on_hbm] * len(held) + [on_vmem] * len(rest),
        out_specs=jax.tree.map(lambda _: on_hbm if out_hbm else on_vmem, out_shape),
        out_shape=out_shape,
        scratch_shapes=scratch,
        compiler_params=pltpu.CompilerParams(vmem_limit_bytes=vmem * MIB),
        cost_estimate=pl.CostEstimate(flops=flops, bytes_accessed=1000, transcendentals=0),
        name=name,
    )(scalars, *held, *rest)


def touch_kernel(scalars_ref, f_ref, out_ref):
    for i in range(scalars_ref.shape[0]):
        out_ref[i] = scalars_ref[i]


def touch(scalars, inv_factor):
    return pl.pallas_call(
        touch_kernel,
        in_specs=[pl.BlockSpec(memory_space=pltpu.SMEM), pl.BlockSpec(memory_space=pltpu.VMEM)],
        out_specs=pl.BlockSpec(memory_space=pltpu.SMEM),
        out_shape=jax.ShapeDtypeStruct(scalars.shape, scalars.dtype),
        compiler_params=pltpu.CompilerParams(vmem_limit_bytes=16 * MIB),
        cost_estimate=pl.CostEstimate(flops=1000, bytes_accessed=1000, transcendentals=0),
        name="touch",
    )(scalars, inv_factor)


def whiten_kernel(blocks, before, scalars_ref, f_ref, *refs):
    earlier, pieces, (keep_ref, away_ref, x_ref, xt_ref) = refs[:before], refs[before:-4], refs[-4:]
    place = 0
    for piece in pieces:
        x_ref[pl.ds(place, piece.shape[0]), :] = piece[...]
        place += piece.shape[0]
    wide = min(512, x_ref.shape[1])
    for c in range(x_ref.shape[1] // wide):
        xt_ref[pl.ds(c * wide, wide), :] = x_ref[:, c * wide:(c + 1) * wide].T
    tile = f_ref.shape[0] // blocks
    done = 0
    if before:
        done = earlier[0].shape[1]
        keep_ref[:, :done] = earlier[0][...]
        away_ref[:, :done] = earlier[1][...]

    def product(t):
        start = pl.multiple_of(scalars_ref[STARTS + t], tile)
        return jnp.dot(f_ref[pl.ds(start, tile), :], xt_ref[...], preferred_element_type=jnp.float32)

    def step(t, carry):
        place = pl.multiple_of(t * tile, tile)
        away_ref[pl.ds(place, tile), done:] = product(blocks // 2 + t).astype(jnp.bfloat16)
        keep_ref[pl.ds(place, tile), done:] = product(t)
        return carry

    lax.fori_loop(0, blocks // 2, step, 0)


def whiten(scalars, blocks, inv_factor, pieces, earlier=()):
    row_block, feat_block = inv_factor.shape
    rows = sum(p.shape[0] for p in pieces)
    out = (row_block // 2, rows + (earlier[0].shape[1] if earlier else 0))
    return call(
        functools.partial(whiten_kernel, blocks, len(earlier)),
        "whiten",
        [jax.ShapeDtypeStruct(out, jnp.float32), jax.ShapeDtypeStruct(out, jnp.bfloat16)],
        [pltpu.VMEM((rows, feat_block), jnp.bfloat16), pltpu.VMEM((feat_block, rows), jnp.bfloat16)],
        (scalars, [inv_factor] + list(earlier) + pieces),
        flops=8 * row_block * feat_block * rows,
    )


def halve_kernel(_, part_ref, got_ref, keep_ref, away_ref):
    left = keep_ref.shape[0]
    keep_ref[...] = part_ref[:left, :] + got_ref[:left, :].astype(jnp.float32)
    away_ref[...] = (part_ref[left:, :] + got_ref[left:, :].astype(jnp.float32)).astype(jnp.bfloat16)


def halve(scalars, part, got):
    out = (part.shape[0] // 2, part.shape[1])
    return call(
        halve_kernel,
        "halve",
        [jax.ShapeDtypeStruct(out, jnp.float32), jax.ShapeDtypeStruct(out, jnp.bfloat16)],
        [],
        (scalars, [part, got]),
    )


def pick_kernel(count, half, scalars_ref, *refs):
    pieces, outs = refs[:count], refs[count:]
    width = outs[0].shape[1]
    start = pl.multiple_of(scalars_ref[BLOCK] * width, width)
    place = 0
    for piece in pieces:
        outs[0][pl.ds(place, piece.shape[0]), :] = piece[:, pl.ds(start, width)]
        place += piece.shape[0]
    if half:
        outs[1][...] = pieces[-1][:half, :]
        for out, piece in zip(outs[2:], pieces):
            out[...] = piece[half:, :]


def pick(scalars, pieces, width, half=0):
    rows = sum(p.shape[0] for p in pieces)
    out = [jax.ShapeDtypeStruct((rows, width), jnp.bfloat16)]
    if half:
        out += [jax.ShapeDtypeStruct((half, pieces[0].shape[1]), jnp.bfloat16)] * len(pieces)
    return call(
        functools.partial(pick_kernel, len(pieces), half), "pick", out, [], (scalars, pieces)
    )


def fetch(pairs, sems):
    copies = [pltpu.make_async_copy(a, b, sems.at[i]) for i, (a, b) in enumerate(pairs)]
    for copy in copies:
        copy.start()
    return copies


def pack_kernel(count, scalars_ref, *refs):
    out_ref, sems = refs[-2:]

    def copy(sources):
        place, pairs = 0, []
        for source in sources:
            pairs.append((source, out_ref.at[pl.ds(place, source.shape[0])]))
            place += source.shape[0]
        for one in fetch(pairs, sems):
            one.wait()

    @pl.when(scalars_ref[NEAR] == 1)
    def _():
        copy(refs[:count])

    @pl.when(scalars_ref[NEAR] == 0)
    def _():
        copy(refs[count:-2])


def pack(scalars, own, got):
    out = (sum(x.shape[0] for x in own), own[0].shape[1])
    return call(
        functools.partial(pack_kernel, len(own)),
        "pack",
        jax.ShapeDtypeStruct(out, jnp.bfloat16),
        [pltpu.SemaphoreType.DMA((len(own),))],
        (scalars, []),
        tuple(own + got),
        BIG,
    )


def join_kernel(first, scalars_ref, own_ref, other_ref, out_ref, x_ref, xt_ref, in_sems, out_sems):
    wide = min(256, x_ref.shape[1])
    parts = [pl.ds(c * wide, wide) for c in range(x_ref.shape[1] // wide)]

    def turn(source):
        arriving = fetch(
            [(source.at[:, pl.ds(first + c * wide, wide)], x_ref.at[:, part]) for c, part in enumerate(parts)],
            in_sems,
        )
        leaving = []
        for c, part in enumerate(parts):
            arriving[c].wait()
            xt_ref[part, :] = x_ref[:, part].T
            leaving += fetch([(xt_ref.at[part], out_ref.at[part])], out_sems.at[pl.ds(c, 1)])
        for one in leaving:
            one.wait()

    @pl.when(scalars_ref[EVEN] == 1)
    def _():
        turn(own_ref)

    @pl.when(scalars_ref[EVEN] == 0)
    def _():
        turn(other_ref)


def join(scalars, own, other, half):
    rows, width = own.shape[0], own.shape[1] // 2
    return call(
        functools.partial(join_kernel, half * width),
        "join",
        jax.ShapeDtypeStruct((width, rows), jnp.bfloat16),
        [
            pltpu.VMEM((rows, width), jnp.bfloat16),
            pltpu.VMEM((width, rows), jnp.bfloat16),
            pltpu.SemaphoreType.DMA((max(1, width // 256),)),
            pltpu.SemaphoreType.DMA((max(1, width // 256),)),
        ],
        (scalars, []),
        (own, other, "out"),
        BIG,
    )


def put_squares(out_ref, scalars_ref, slot, part_ref, other_ref):
    count = out_ref.shape[1]
    value = part_ref[...] + other_ref[...].astype(jnp.float32)
    line = jnp.sum(value * value, axis=0, keepdims=True)
    for i in range(line.shape[1] // count):
        out_ref[pl.ds(scalars_ref[slot + i], 1), :] = line[:, i * count:(i + 1) * count]


def early_kernel(slots, firsts, scalars_ref, w_ref, strata_ref, *refs):
    out_ref = refs[-1]
    out_ref[...] = jnp.zeros_like(out_ref)

    @pl.when(scalars_ref[FEAT] == 0)
    def _():
        out_ref[pl.ds(slots + scalars_ref[ROW], 1), :] = w_ref[...]
        out_ref[pl.ds(2 * slots + scalars_ref[ROW], 1), :] = strata_ref[...].astype(jnp.float32)

    for g, first in enumerate(firsts):
        put_squares(out_ref, scalars_ref, first, refs[2 * g], refs[2 * g + 1])


def early_squares(scalars, firsts, slots, weights, strata, pairs):
    return call(
        functools.partial(early_kernel, slots, firsts),
        "early_squares",
        jax.ShapeDtypeStruct((3 * slots, weights.shape[1]), jnp.float32),
        [],
        (scalars, [weights, strata] + [x for pair in pairs for x in pair]),
    )


def last_kernel(first, scalars_ref, sums_ref, keep_ref, got_ref, out_ref):
    out_ref[...] = sums_ref[...]
    put_squares(out_ref, scalars_ref, first, keep_ref, got_ref)


def last_squares(scalars, first, sums, pair):
    return call(
        functools.partial(last_kernel, first),
        "last_squares",
        jax.ShapeDtypeStruct(sums.shape, jnp.float32),
        [],
        (scalars, [sums] + list(pair)),
    )


def weight_step(strata_n, features, row, sums_ref, new_ref, lev_ref, all_ref, d_ref):
    groups = sums_ref.shape[0] // 3
    raw, weights, strata = [sums_ref[pl.ds(i * groups, groups), :] for i in range(3)]
    products = weights * raw
    ratio = jnp.zeros_like(raw)
    for s in range(strata_n):
        inside = strata == float(s)
        mass = jnp.sum(jnp.where(inside, weights, 0.0), keepdims=True)
        product = jnp.sum(jnp.where(inside, products, 0.0), keepdims=True)
        ratio = jnp.where(inside, mass / product, ratio)
    new = products * ratio
    all_ref[...] = new
    new_ref[...] = all_ref[pl.ds(row, 1), :]
    lev_ref[...] = sums_ref[pl.ds(row, 1), :] / features
    step = new - weights
    count = step.shape[1]
    for g in range(groups):
        d_ref[pl.ds(g * count, count), :] = jnp.broadcast_to(step[g:g + 1, :], (LANES, count)).T


def information_kernel(features, pieces_of, scalars_ref, low_hbm, high_hbm, *refs):
    n = len(pieces_of)
    pieces, (sums_ref, got_ref, out_ref, new_ref, lev_ref) = refs[:n], refs[n:n + 5]
    all_ref, total_ref, d_ref, col_ref, p_ref, s_ref, buf_ref, col_sems, first_sems, rest_sems, sems = refs[n + 5:]
    width = s_ref.shape[1]
    steps = out_ref.shape[1] // width
    count = sums_ref.shape[1]
    sizes = [piece.shape[0] for piece in pieces]
    offsets = [sum(sizes[:i]) for i in range(n)]

    def bring(start, size):
        columns = pl.ds(start, size)
        return [
            (piece.at[:, columns], p_ref.at[pl.ds(offset, rows), columns])
            for piece, offset, rows in zip(pieces, offsets, sizes)
        ]

    def copy(j):
        slot = lax.rem(j, 2)
        return pltpu.make_async_copy(
            buf_ref.at[slot], out_ref.at[:, pl.ds(pl.multiple_of(j * width, width), width)], sems.at[slot]
        )

    half = col_ref.shape[0] // 2
    first = fetch(bring(0, width), first_sems)
    first += fetch([(low_hbm, col_ref.at[:half]), (high_hbm, col_ref.at[half:])], col_sems)
    total_ref[...] = sums_ref[...] + got_ref[...]
    weight_step(
        2 * (sums_ref.shape[0] // 3), features, scalars_ref[ROW], total_ref, new_ref, lev_ref, all_ref, d_ref
    )
    for one in first:
        one.wait()
    rest = fetch(bring(width, (steps - 1) * width), rest_sems) if steps > 1 else []

    def step(j, carry):
        @pl.when(j == 1)
        def _():
            for one in rest:
                one.wait()

        for i, (slot, first) in enumerate(pieces_of):
            size = sizes[i]
            start = pl.multiple_of(scalars_ref[slot] * count + first, size)
            scale = d_ref[pl.ds(start, size), :]
            for c in range(width // LANES):
                start = pl.multiple_of(j * width + c * LANES, LANES)
                value = p_ref[pl.ds(offsets[i], size), pl.ds(start, LANES)].astype(jnp.float32)
                s_ref[pl.ds(offsets[i], size), c * LANES:(c + 1) * LANES] = (scale * value).astype(jnp.bfloat16)

        @pl.when(j > 1)
        def _():
            copy(j - 2).wait()

        buf_ref[lax.rem(j, 2)] = jnp.dot(col_ref[...], s_ref[...], preferred_element_type=jnp.float32)
        copy(j).start()
        return carry

    lax.fori_loop(0, steps, step, 0)
    for j in range(max(0, steps - 2), steps):
        copy(jnp.int32(j)).wait()


def increment(scalars, pieces_of, sums, got, columns_t, pieces, features):
    row_block, rows = 2 * columns_t[0].shape[0], columns_t[0].shape[1]
    groups, count = sums.shape[0] // 3, sums.shape[1]
    feat_block = pieces[0].shape[1]
    width = min(256, feat_block)
    steps = feat_block // width
    on_vmem = pl.BlockSpec(memory_space=pltpu.VMEM)
    on_hbm = pl.BlockSpec(memory_space=pltpu.HBM)
    return pl.pallas_call(
        functools.partial(information_kernel, features, pieces_of),
        in_specs=[pl.BlockSpec(memory_space=pltpu.SMEM)] + [on_hbm] * (2 + len(pieces)) + [on_vmem] * 2,
        out_specs=[on_hbm, on_vmem, on_vmem],
        out_shape=[
            jax.ShapeDtypeStruct((row_block, feat_block), jnp.float32),
            jax.ShapeDtypeStruct((1, count), jnp.float32),
            jax.ShapeDtypeStruct((1, count), jnp.float32),
        ],
        scratch_shapes=[
            pltpu.VMEM((groups, count), jnp.float32),
            pltpu.VMEM((3 * groups, count), jnp.float32),
            pltpu.VMEM((rows, LANES), jnp.float32),
            pltpu.VMEM((row_block, rows), jnp.bfloat16),
            pltpu.VMEM((rows, feat_block), jnp.bfloat16),
            pltpu.VMEM((rows, width), jnp.bfloat16),
            pltpu.VMEM((2, row_block, width), jnp.float32),
            pltpu.SemaphoreType.DMA((2,)),
            pltpu.SemaphoreType.DMA((len(pieces),)),
            pltpu.SemaphoreType.DMA((len(pieces),)),
            pltpu.SemaphoreType.DMA((2,)),
        ],
        compiler_params=pltpu.CompilerParams(vmem_limit_bytes=BIG * MIB),
        cost_estimate=pl.CostEstimate(
            flops=2 * row_block * feat_block * rows, bytes_accessed=1000, transcendentals=0
        ),
        name="increment",
    )(scalars, *columns_t, *pieces, sums, got)


def make(mesh):
    rows_n, feats_n = mesh.shape["row"], mesh.shape["feat"]
    hi_n = HI
    lo_n = rows_n // hi_n
    per_feat = rows_n // feats_n
    everyone = [(r, f) for r in range(rows_n) for f in range(feats_n)]

    def perm(target, keep=lambda r, f: True):
        out = []
        for r, f in everyone:
            if keep(r, f):
                r2, f2 = target(r, f)
                out.append((r * feats_n + f, r2 * feats_n + f2))
        return out

    def send(x, pairs):
        return lax.ppermute(x, BOTH, pairs)

    def swap(x, r_bit, f_bit):
        return send(x, perm(lambda r, f: (r ^ r_bit, f ^ f_bit)))

    fence = lax.optimization_barrier
    hi_next, lo_next = ring_next(hi_n), ring_next(lo_n)
    hi_pairs = perm(lambda r, f: (hi_next[r // lo_n] * lo_n + r % lo_n, f))
    lo_pairs = perm(lambda r, f: (r // lo_n * lo_n + lo_next[r % lo_n], f))
    hi_order, lo_order = ring_order(hi_n), ring_order(lo_n)

    def source(r, k, s):
        h, l = r // lo_n, r % lo_n
        h2 = hi_order[(hi_order.index(h) - k) % hi_n]
        l2 = lo_order[(lo_order.index(l) - s) % lo_n]
        return h2 * lo_n + l2

    feat_bits = [1 << b for b in range(feats_n.bit_length() - 1)]
    far_bits = feat_bits[1:]
    row_bits = [1 << b for b in range(rows_n.bit_length() - 1)]
    relative = [0]
    for bit in reversed(feat_bits):
        relative = relative + [j + bit for j in relative]

    groups = [[(0, s) for s in range(lo_n)] + [(1, 0)]]
    for k in range(1, hi_n):
        groups.append([(k, s) for s in range(1, lo_n)] + ([(k + 1, 0)] if k + 1 < hi_n else []))
    slots = [slot for group in groups for slot in group]
    white_groups = [[(k, s) for k in ks for s in range(lo_n)] for ks in [[0, 1]] + [[k] for k in range(2, hi_n)]]
    white_slots = [slot for group in white_groups for slot in group]

    def per_device(candidates, inv_factor, weights, strata):
        rows_dev, feat_block = candidates.shape
        row_block = inv_factor.shape[0]
        features = feat_block * feats_n
        half = rows_dev // 2
        row, feat = lax.axis_index("row"), lax.axis_index("feat")
        def sources(chosen):
            table = [[source(r, *slot) for slot in chosen] for r in range(rows_n)]
            return jnp.asarray(table, jnp.int32)[row]

        apart = feat ^ (row // per_feat)
        fixed = [row % per_feat, apart == 0, apart % 2 == 0, row, feat]
        scalars = jnp.concatenate([
            jnp.stack([jnp.asarray(x, jnp.int32) for x in fixed]),
            (jnp.asarray(relative, jnp.int32) ^ feat) * (row_block // feats_n),
            sources(slots),
            sources(white_slots),
        ])
        first_place = STARTS + feats_n
        first_white = first_place + rows_n

        def pieces_of(chosen):
            return [p for slot in chosen for p in chunks[slot]]

        def column_far(mine):
            for bit in reversed(far_bits):
                got = send(mine, perm(
                    lambda r, f: (r, f ^ bit),
                    lambda r, f: (f ^ (r // per_feat)) % (2 * bit) == 0,
                ))
                if len(far_bits) > 1:
                    mine = got = jnp.where(apart % (2 * bit) == 0, mine, got)
            return got

        def to_far(near):
            keep, away = halve(scalars, *near)
            for bit in far_bits[:-1]:
                keep, away = halve(scalars, keep, swap(away, 0, bit))
            return keep, swap(away, 0, far_bits[-1])

        chunks = {(0, 0): [candidates]}
        columns, far_columns, white, near, far = [], [], [], [], []
        for k in range(hi_n + 1):
            fresh, out = [], {}
            if k > 0:
                last = k == hi_n - 1
                picked = pick(scalars, pieces_of(groups[k - 1]), row_block, half if last else 0)
                columns.append(picked[0])
            if k < hi_n - 1:
                fresh.append((k + 1, 0))
                chunks[k + 1, 0] = [send(chunks[k, 0][0], hi_pairs)]
                held = chunks[k, 0][0]
                for s in range(1, lo_n):
                    fresh.append((k, s))
                    held = send(held, lo_pairs)
                    chunks[k, s] = [held]
            elif k < hi_n:
                held = picked[1]
                for s in range(1, lo_n):
                    fresh.append((k, s))
                    held = send(held, lo_pairs)
                    chunks[k, s] = [held, send(picked[1 + s], hi_pairs)]
            out["fresh"] = [chunks[slot] for slot in fresh]
            if k == 0:
                out["scalars"] = touch(scalars, inv_factor)
            if k > 0:
                out["column"] = column_far(columns[-1])
                white_pieces = pieces_of([(k - 1, s) for s in range(lo_n)])
                earlier = white.pop() if k == 2 else ()
                out["white"] = whiten(scalars, feats_n, inv_factor, white_pieces, earlier)
            if k > 2:
                keep, away = white[k - 3]
                out["near"] = keep, swap(away, 0, 1)
            if k > 3:
                out["far"] = to_far(near[k - 4])
            out = fence(out)
            for slot, value in zip(fresh, out["fresh"]):
                chunks[slot] = value
            scalars = out.get("scalars", scalars)
            for name, kept in (("column", far_columns), ("white", white), ("near", near), ("far", far)):
                if name in out:
                    kept.append(out[name])
        keep, away = white[-1]
        packed = pack(scalars, columns, far_columns)
        last, before, packed = fence(((keep, swap(away, 0, 1)), to_far(near[-1]), packed))
        far.append(before)
        slots_n = len(white_slots)
        firsts = [first_white + sum(len(x) for x in white_groups[:g]) for g in range(len(white_groups))]
        sums = early_squares(scalars, firsts[:-1], slots_n, weights[None], strata[None], far)
        last, beside, sums = fence((to_far(last), swap(packed, 0, 1), sums))
        total = last_squares(scalars, firsts[-1], sums, last)
        total = fence(total + swap(total, 0, 1))
        columns_t = []
        bits = [(0, bit) for bit in far_bits] + [(bit, 0) for bit in row_bits]
        for bit in bits[:-1]:
            total = total + swap(total, *bit)
            if len(columns_t) < 2:
                columns_t.append(join(scalars, packed, beside, len(columns_t)))
                total, columns_t = fence((total, columns_t))
        got = swap(total, *bits[-1])
        origins = []
        for i, slot in enumerate(slots):
            first = 0
            for piece in chunks[slot]:
                origins.append((first_place + i, first))
                first += piece.shape[0]
        information, new_weight, leverage = increment(
            scalars, origins, total, got, columns_t, pieces_of(slots), features
        )
        return (new_weight.reshape(rows_dev), leverage.reshape(rows_dev), information)

    return per_device


def solution(mesh):
    in_specs = (P("row", "feat"), P("row", "feat"), P("row"), P("row"))
    out_specs = (P("row"), P("row"), P("row", "feat"))
    return jax.shard_map(
        make(mesh), mesh=mesh, in_specs=in_specs, out_specs=out_specs, check_vma=False
    )
```
